512 devices in a mesh: mp: 16 (over z_lo, y), dp: 32 (over z_hi, x, core).
Axes of the slice: x: 4, y: 4, z: 16 (z_hi: 4, z_lo: 4; z = z_hi * 4 + z_lo), core: 2. Of those that a mesh axis runs over, the one named last changes fastest.
Arguments:
- train_acts: bfloat16 [16, 128, 64, 3584], P('mp', 'dp'), may hold values from -6 to 6
- train_grads: bfloat16 [16, 128, 64, 2048], P('mp', 'dp'), may hold values from -6 to 6
- query_acts: bfloat16 [16, 64, 64, 3584], P('mp', 'dp'), may hold values from -6 to 6
- query_grads: bfloat16 [16, 64, 64, 2048], P('mp', 'dp'), may hold values from -6 to 6
- train_lengths: int32 [128], P('dp'), may hold values from 8 to 64, as said below
- query_lengths: int32 [64], P('dp'), may hold values from 8 to 64, as said below
- proj_salts: int32 [16, 2], P('mp'), may hold values from 0 to 99999
Outputs:
- scores: float32 [64, 128], P('dp', 'mp')
The draws below stay inside these ranges and needn't reach their ends.
Inputs may be any that keep to these rules, and one draw needn't show every extreme that they name: `train_lengths`: some training example uses all 64 slots and some uses 64 // 8. `query_lengths`: some query example uses all 64 slots and some uses 64 // 8.
All inputs are finite; a program needn't handle non-finite values.
Results may differ from the reference program's by a relative error of at most 0.0003.
Values sent between devices are 32-bit elements; how exact they have to be, the bound alone decides.
A program may use at most 64 MiB of HBM per device.

```python
import jax
import jax.numpy as jnp
from jax import lax

D = 3584
KV = 2048
R1 = 64
R2 = 64
LEN = 64
CKPT = 16
TRAIN = 128
QUERIES = 64


def draw_train_lengths(key, part):
    key = jax.random.fold_in(key, 11)
    values = jax.random.randint(key, (TRAIN,), LEN // 8, LEN + 1, dtype=jnp.int32)
    return values.at[0].set(LEN).at[TRAIN - 1].set(LEN // 8)


def draw_query_lengths(key, part):
    key = jax.random.fold_in(key, 23)
    values = jax.random.randint(key, (QUERIES,), LEN // 8, LEN + 1, dtype=jnp.int32)
    return values.at[0].set(LEN).at[QUERIES - 1].set(LEN // 8)


def set_ends(drawn, key, smallest, largest):
    longest = drawn.shape.index(max(drawn.shape))
    spots = []
    for shift in (0, 1):
        where = [jax.random.randint(jax.random.fold_in(key, axis), (), 0, length) for axis, length in enumerate(drawn.shape)]
        where[longest] = (where[longest] + shift) % drawn.shape[longest]
        spots.append(tuple(where))
    return drawn.at[spots[0]].set(smallest).at[spots[1]].set(largest)


def steps_of(stream_key, shape, pieces, low, top_value):
    loudness, own = 1.0, jax.random.fold_in(stream_key, 6)
    for position, blocks in pieces:
        draws = jnp.exp(jax.random.uniform(jax.random.fold_in(own, position), (blocks,), jnp.float32, low / len(pieces), top_value / len(pieces)))
        loudness = loudness * jnp.repeat(draws, shape[position] // blocks).reshape([-1 if axis == position else 1 for axis in range(len(shape))])
    return loudness


def centred(key, dims, scale, bound, cuts=(), kind=jnp.bfloat16):
    values = jax.random.normal(key, dims, jnp.float32) * scale
    if len(cuts) > 0:
        values = steps_of(key, dims, cuts, -0.22, 0.18) * values
    return jnp.clip(values, min=-bound, max=bound).astype(kind)


def setup_inputs(seed: int = 0) -> dict:
    key_of = jax.random.split(jax.random.key(seed), 8)
    train_acts = centred(key_of[0], (CKPT, TRAIN, LEN, D), 1.0, 6.0, ((0, 16), (1, 32)))
    train_grads = centred(key_of[1], (CKPT, TRAIN, LEN, KV), 1.0, 6.0, ((0, 16), (1, 32)))
    query_acts = centred(key_of[2], (CKPT, QUERIES, LEN, D), 1.0, 6.0, ((0, 16), (1, 32)))
    query_grads = centred(key_of[3], (CKPT, QUERIES, LEN, KV), 1.0, 6.0, ((0, 16), (1, 32)))
    train_lengths = draw_train_lengths(jax.random.fold_in(key_of[7], 71), 0)
    query_lengths = draw_query_lengths(jax.random.fold_in(key_of[7], 71), 0)
    proj_salts = set_ends(jax.random.randint(key_of[6], (CKPT, 2), 0, 100000), jax.random.fold_in(key_of[6], 1), 0, 99999).astype(jnp.int32)
    return dict(train_acts=train_acts, train_grads=train_grads, query_acts=query_acts, query_grads=query_grads, train_lengths=train_lengths, query_lengths=query_lengths, proj_salts=proj_salts)


RIDGE_SCALE = 0.1

def shift_down(value, amount):
    return lax.shift_right_logical(value, jnp.full_like(value, amount))

def sign_table(hash_salt, rows, cols):
    row_index = lax.broadcasted_iota(jnp.int32, (rows, cols), 0)
    col_index = lax.broadcasted_iota(jnp.int32, (rows, cols), 1)
    hashed = row_index * 73856093 + col_index * 19349663 + hash_salt.astype(jnp.int32) * 83492791
    hashed = hashed ^ shift_down(hashed, 15)
    hashed = hashed * 1274126177
    hashed = hashed ^ shift_down(hashed, 13)
    hashed = hashed * 668265263
    hashed = hashed ^ shift_down(hashed, 16)
    bit_value = shift_down(hashed, 7) & 1
    signs = (bit_value * 2 - 1).astype(jnp.float32)
    return (signs * (1.0 / rows ** 0.5)).astype(jnp.bfloat16)

def project(activations, gradients, lengths, proj_in, proj_out):
    count, length, width = activations.shape
    left = jnp.dot(activations.reshape(count * length, width).astype(jnp.float32), proj_in.astype(jnp.float32), preferred_element_type=jnp.float32)
    right = jnp.dot(gradients.reshape(count * length, gradients.shape[2]).astype(jnp.float32), proj_out.astype(jnp.float32), preferred_element_type=jnp.float32)
    left = left.reshape(count, length, proj_in.shape[1])
    right = right.reshape(count, length, proj_out.shape[1])
    positions = lax.broadcasted_iota(jnp.int32, (count, length), 1)
    token_mask = (positions < lengths.astype(jnp.int32)[:, None]).astype(jnp.float32)
    left = left * token_mask[:, :, None]
    outer = jnp.einsum('elr,els->ers', left, right, precision=lax.Precision.HIGHEST)
    return outer.reshape(count, proj_in.shape[1] * proj_out.shape[1])

def reference(train_acts, train_grads, query_acts, query_grads, train_lengths, query_lengths, proj_salts):
    total = jnp.zeros((QUERIES, TRAIN), jnp.float32)
    for which in range(CKPT):
        proj_in = sign_table(proj_salts[which, 0], D, R1)
        proj_out = sign_table(proj_salts[which, 1], KV, R2)
        train_rows = project(train_acts[which], train_grads[which], train_lengths, proj_in, proj_out)
        query_rows = project(query_acts[which], query_grads[which], query_lengths, proj_in, proj_out)
        kernel = jnp.dot(train_rows.astype(jnp.float32), train_rows.T.astype(jnp.float32), precision=lax.Precision.HIGHEST, preferred_element_type=jnp.float32)
        cross_terms = jnp.dot(query_rows.astype(jnp.float32), train_rows.T.astype(jnp.float32), precision=lax.Precision.HIGHEST, preferred_element_type=jnp.float32)
        ridge_term = RIDGE_SCALE * jnp.trace(kernel) / TRAIN
        system = kernel + ridge_term * jnp.eye(TRAIN, dtype=jnp.float32)
        factor = jnp.linalg.cholesky(system)
        solved = jax.scipy.linalg.cho_solve((factor, True), cross_terms.T).T
        total = total + solved
    return total * (TRAIN / CKPT)
```

```python
import functools

import jax
import jax.numpy as jnp
from jax import lax
from jax.experimental import pallas as pl
from jax.experimental.pallas import tpu as pltpu
from jax.sharding import PartitionSpec as P

MESH = pl.DeviceIdType.MESH
R1 = 64
R2 = 64
RIDGE_SCALE = 0.1
LANES = 128
TILE = 8
PLANES = 4
SPOTS = 8
SLICE_ROWS = 4


def sign_table(salt, rows, table_ref):
    half = rows // 2
    row = lax.broadcasted_iota(jnp.int32, (LANES, LANES), 0)
    lane = lax.broadcasted_iota(jnp.int32, (LANES, LANES), 1)
    row = row + jnp.where(lane >= R1, half, 0)
    base = row * 73856093 + (lane & (R1 - 1)) * 19349663 + salt * 83492791
    scale = 1.0 / rows**0.5

    def chunk(step, carry):
        h = base + step * LANES * 73856093
        h = h ^ lax.shift_right_logical(h, 15)
        h = h * 1274126177
        h = h ^ lax.shift_right_logical(h, 13)
        h = h * 668265263
        bit = (lax.shift_right_logical(h, 16) ^ h) & 128
        signs = jnp.where(bit != 0, scale, -scale).astype(jnp.bfloat16)
        table_ref[pl.ds(pl.multiple_of(step * LANES, LANES), LANES), :] = signs
        return carry

    lax.fori_loop(0, half // LANES, chunk, 0, unroll=2)


def projected(tokens, table):
    half = table.shape[0]
    upper = jnp.dot(tokens[:, :half], table, preferred_element_type=jnp.float32)
    lower = jnp.dot(tokens[:, half:], table, preferred_element_type=jnp.float32)
    return upper[:, :R1] + lower[:, R1:]


def rows_by_columns(first, second):
    return lax.dot_general(
        first,
        second,
        (((1,), (1,)), ((), ())),
        precision=lax.Precision.HIGHEST,
        preferred_element_type=jnp.float32,
    )


def features(left, right, length):
    position = lax.broadcasted_iota(jnp.int32, left.shape, 0)
    left = jnp.where(position < length, left, 0.0)
    outer = lax.dot_general(
        left,
        right,
        (((0,), (0,)), ((), ())),
        precision=lax.Precision.HIGHEST,
        preferred_element_type=jnp.float32,
    )
    return jnp.concatenate([outer[: R1 // 2], outer[R1 // 2 :]], axis=1)


def solve(gram, rhs):
    total = gram.shape[0]
    lane = lax.broadcasted_iota(jnp.int32, (TILE, LANES), 1)
    blocks = total // TILE

    def spread(tile, column):
        return jnp.broadcast_to(tile[:, column : column + 1], (TILE, LANES))

    def down(tile, row):
        return jnp.broadcast_to(tile[row : row + 1, :], (TILE, LANES))

    def step(_, tiles):
        pivot, others = tiles[0], tiles[1:]
        columns = [spread(pivot, t) for t in range(TILE)]
        entry = {(k, t): down(columns[t], k) for t in range(TILE) for k in range(t + 1)}
        row = [jnp.where(lane == k, -1.0, jnp.where(lane < TILE, 0.0, down(pivot, k))) for k in range(TILE)]
        for t in range(TILE):
            inverse = 1.0 / entry[t, t]
            row[t] = row[t] * inverse
            scaled = {l: entry[t, l] * inverse for l in range(t + 1, TILE)}
            for k in range(TILE):
                if k == t:
                    continue
                factor = entry[t, k] if k > t else entry[k, t]
                row[k] = row[k] - factor * row[t]
                for l in range(t + 1, TILE):
                    if k < t or l >= k:
                        entry[k, l] = entry[k, l] - factor * scaled[l]
            for l in range(t + 1, TILE):
                entry[t, l] = scaled[l]
        changed = []
        for tile in others:
            terms = [spread(tile, k) * row[k] for k in range(TILE)]
            while len(terms) > 1:
                terms = [a + b for a, b in zip(terms[::2], terms[1::2])]
            tile = jnp.where(lane < TILE, 0.0, tile) - terms[0]
            changed.append(pltpu.roll(tile, LANES - TILE, 1))
        return (*changed[:-1], jnp.zeros_like(pivot), changed[-1])

    tiles = tuple(gram[TILE * b : TILE * (b + 1)] for b in range(blocks)) + (rhs,)
    return lax.fori_loop(0, blocks, step, tiles)[-1]


def kernel(
    salts, train_lengths, query_lengths, train_acts, train_grads, query_acts, query_grads, out_ref,
    acts, grads, table_in, table_out, train_send, query_send, train_recv, query_recv,
    gram_part, cross_part, gram_recv, cross_recv, gram_row, gram_full, score_send, score_recv, result_send, result_recv,
    load_sems, send_sems, recv_sems,
):
    dp, mp = lax.axis_index("dp"), lax.axis_index("mp")
    members, ckpts = lax.axis_size("dp"), lax.axis_size("mp")
    trains, queries = train_acts.shape[1], query_acts.shape[1]
    spot = lax.rem(dp, SPOTS)
    home = dp < SPOTS

    loads = [
        pltpu.make_async_copy(train_grads.at[0], grads.at[pl.ds(0, trains)], load_sems.at[0]),
        pltpu.make_async_copy(query_grads.at[0], grads.at[pl.ds(trains, queries)], load_sems.at[1]),
        pltpu.make_async_copy(train_acts.at[0], acts.at[pl.ds(0, trains)], load_sems.at[2]),
        pltpu.make_async_copy(query_acts.at[0], acts.at[pl.ds(trains, queries)], load_sems.at[3]),
    ]
    for load in loads:
        load.start()

    barrier = pltpu.get_barrier_semaphore()

    def greet_dp(peer):
        pl.semaphore_signal(barrier, inc=1, device_id={"dp": peer}, device_id_type=MESH)

    def greet_mp(peer):
        pl.semaphore_signal(barrier, inc=1, device_id={"mp": peer}, device_id_type=MESH)

    def send(phase, source, target, device):
        copy = pltpu.make_async_remote_copy(
            src_ref=source, dst_ref=target, send_sem=send_sems.at[phase], recv_sem=recv_sems.at[phase],
            device_id=device, device_id_type=MESH,
        )
        copy.start()

    def sent(phase, like):
        pltpu.make_async_copy(like, like, send_sems.at[phase]).wait()

    def received(phase, like):
        pltpu.make_async_copy(like, like, recv_sems.at[phase]).wait()

    @pl.when(home)
    def _():
        @pl.loop(1, members)
        def _(k):
            greet_dp(lax.rem(dp + k, members))

        @pl.loop(1, ckpts)
        def _(k):
            greet_mp(lax.rem(mp + k, ckpts))

    @pl.when(jnp.logical_not(home))
    def _():
        @pl.loop(0, SPOTS)
        def _(k):
            greet_dp(k)

    sign_table(salts[0, 1], grads.shape[2], table_out)
    sign_table(salts[0, 0], acts.shape[2], table_in)

    count, length = acts.shape[0], acts.shape[1]
    loads[0].wait()
    loads[1].wait()
    right = projected(grads[...].reshape(count * length, grads.shape[2]), table_out[...])
    loads[2].wait()
    loads[3].wait()
    left = projected(acts[...].reshape(count * length, acts.shape[2]), table_in[...])
    for e in range(count):
        tokens = slice(e * length, (e + 1) * length)
        tokens_used = train_lengths[e] if e < trains else query_lengths[e - trains]
        rows = features(left[tokens], right[tokens], tokens_used)
        rows = rows.reshape(SPOTS, SLICE_ROWS, LANES)
        if e < trains:
            for j in range(SLICE_ROWS):
                train_send[:, j // 2, (j % 2) * trains + e, :] = rows[:, j]
        else:
            for j in range(SLICE_ROWS):
                query_send[:, j * queries + e - trains, :] = rows[:, j]

    def spread_features(first):
        @pl.loop(first, SPOTS)
        def _(k):
            to = lax.rem(spot + k, SPOTS)
            send(0, train_send.at[to], train_recv.at[dp], {"dp": to})

        @pl.loop(first, SPOTS)
        def _(k):
            to = lax.rem(spot + k, SPOTS)
            send(1, query_send.at[to], query_recv.at[dp], {"dp": to})

    @pl.when(jnp.logical_not(home))
    def _():
        pl.semaphore_wait(barrier, SPOTS)
        spread_features(0)
        received(6, result_recv)
        out_ref[...] = result_recv[0:queries, 0 : out_ref.shape[1]]
        sent(0, train_send)
        sent(1, query_send)

    @pl.when(home)
    def _():
        pl.semaphore_wait(barrier, members - 1 + ckpts - 1)
        spread_features(1)
        train_recv[dp] = train_send[spot]
        query_recv[dp] = query_send[spot]
        others = pl.ds(0, members - 1)
        received(0, train_recv.at[others])

        low = lax.broadcasted_iota(jnp.int32, (members // 2, TILE, LANES), 1) < trains
        train_rows = []
        for j in range(SLICE_ROWS // 2):
            pairs = train_recv[:, j].reshape(members // 2, 2, TILE, LANES)
            even, odd = pairs[:, 0], pairs[:, 1]
            train_rows.append(jnp.where(low, even, pltpu.roll(odd, trains, 1)))
            train_rows.append(jnp.where(low, pltpu.roll(even, trains, 1), odd))
        train_rows = [rows.reshape(members * trains, LANES) for rows in train_rows]
        gram = rows_by_columns(train_rows[0], train_rows[0])
        for rows in train_rows[1:]:
            gram = gram + rows_by_columns(rows, rows)
        gram_part[...] = gram
        share = members * trains // SPOTS

        @pl.loop(1, SPOTS)
        def _(k):
            to = lax.rem(spot + k, SPOTS)
            send(2, gram_part.at[pl.ds(pl.multiple_of(to * share, share), share)], gram_recv.at[spot], {"dp": to})

        gram_recv[spot] = gram_part[pl.ds(pl.multiple_of(spot * share, share), share), :]

        received(1, query_recv.at[others])
        planes = query_recv[...].reshape(PLANES, SPOTS, TILE, LANES)
        position = lax.broadcasted_iota(jnp.int32, (SPOTS, TILE, LANES), 1) // queries
        cross = None
        for j in range(SLICE_ROWS):
            rows = jnp.zeros((SPOTS, TILE, LANES), jnp.float32)
            for plane in range(PLANES):
                shift = (queries * (plane - j)) % TILE
                moved = pltpu.roll(planes[plane], shift, 1) if shift else planes[plane]
                rows = jnp.where(position == plane, moved, rows)
            term = rows_by_columns(rows.reshape(SPOTS * TILE, LANES), train_rows[j])
            cross = term if cross is None else cross + term
        cross_part[...] = cross.reshape(SPOTS, TILE, LANES)

        @pl.loop(1, SPOTS)
        def _(k):
            to = lax.rem(spot + k, SPOTS)
            send(3, cross_part.at[to], cross_recv.at[spot], {"dp": to})

        cross_recv[spot] = cross_part[spot]

        rest = pl.ds(0, SPOTS - 1)
        received(2, gram_recv.at[rest])
        gram_row[...] = jnp.sum(gram_recv[...], axis=0)
        mine = pl.ds(pl.multiple_of(spot * share, share), share)

        @pl.loop(1, SPOTS)
        def _(k):
            send(4, gram_row, gram_full.at[mine], {"dp": lax.rem(spot + k, SPOTS)})

        gram_full[mine, :] = gram_row[...]
        received(3, cross_recv.at[rest])
        cross_terms = jnp.sum(cross_recv[...], axis=0)
        received(4, gram_full.at[pl.ds(0, share * (SPOTS - 1))])

        gram = gram_full[...]
        total = gram.shape[0]
        diagonal = lax.broadcasted_iota(jnp.int32, gram.shape, 0) == lax.broadcasted_iota(jnp.int32, gram.shape, 1)
        trace = jnp.sum(jnp.where(diagonal, gram, 0.0), axis=(0, 1), keepdims=True)
        ridge = RIDGE_SCALE * trace / total
        system = jnp.where(diagonal, gram + ridge, gram)
        solved = solve(system, cross_terms)

        score_send[...] = solved

        @pl.loop(1, ckpts)
        def _(k):
            send(5, score_send, score_recv.at[mp], {"mp": lax.rem(mp + k, ckpts)})

        score_recv[mp] = solved
        received(5, score_recv.at[pl.ds(0, ckpts - 1)])
        summed = jnp.sum(score_recv[...], axis=0) * (total / ckpts)
        width = out_ref.shape[1]
        summed = pltpu.roll(summed, lax.rem((ckpts - mp) * width, LANES), 1)
        for plane in range(1, PLANES):
            result_send[plane, 0:queries, :] = summed[plane * queries : (plane + 1) * queries]
            result_send[plane, queries:, :] = jnp.zeros((TILE - queries, LANES), jnp.float32)
            send(6, result_send.at[plane], result_recv, {"dp": plane * SPOTS + spot})
        out_ref[...] = summed[0:queries, 0:width]
        sent(0, train_send.at[rest])
        sent(1, query_send.at[rest])
        sent(2, gram_recv.at[rest])
        sent(3, cross_recv.at[rest])
        sent(4, gram_full.at[pl.ds(0, share * (SPOTS - 1))])
        sent(5, score_recv.at[pl.ds(0, ckpts - 1)])
        sent(6, result_send.at[pl.ds(0, PLANES - 1)])


def shards(train_acts, train_grads, query_acts, query_grads, train_lengths, query_lengths, proj_salts):
    _, trains, length, width = train_acts.shape
    queries, out_width = query_acts.shape[1], train_grads.shape[3]
    members, ckpts = lax.axis_size("dp"), lax.axis_size("mp")
    total = trains * members
    f32, bf16 = jnp.float32, jnp.bfloat16
    smem, hbm = pl.BlockSpec(memory_space=pltpu.SMEM), pl.BlockSpec(memory_space=pl.ANY)
    return pl.pallas_call(
        kernel,
        out_shape=jax.ShapeDtypeStruct((queries, total // ckpts), f32),
        in_specs=[smem] * 3 + [hbm] * 4,
        out_specs=pl.BlockSpec(memory_space=pltpu.VMEM),
        scratch_shapes=[
            pltpu.VMEM((trains + queries, length, width), bf16),
            pltpu.VMEM((trains + queries, length, out_width), bf16),
            pltpu.VMEM((width // 2, LANES), bf16),
            pltpu.VMEM((out_width // 2, LANES), bf16),
            pltpu.VMEM((SPOTS, SLICE_ROWS // 2, TILE, LANES), f32),
            pltpu.VMEM((SPOTS, TILE, LANES), f32),
            pltpu.VMEM((members, SLICE_ROWS // 2, TILE, LANES), f32),
            pltpu.VMEM((members, TILE, LANES), f32),
            pltpu.VMEM((total, LANES), f32),
            pltpu.VMEM((SPOTS, TILE, LANES), f32),
            pltpu.VMEM((SPOTS, total // SPOTS, LANES), f32),
            pltpu.VMEM((SPOTS, TILE, LANES), f32),
            pltpu.VMEM((total // SPOTS, LANES), f32),
            pltpu.VMEM((total, LANES), f32),
            pltpu.VMEM((TILE, LANES), f32),
            pltpu.VMEM((ckpts, TILE, LANES), f32),
            pltpu.VMEM((PLANES, TILE, LANES), f32),
            pltpu.VMEM((TILE, LANES), f32),
            pltpu.SemaphoreType.DMA((4,)),
            pltpu.SemaphoreType.DMA((7,)),
            pltpu.SemaphoreType.DMA((7,)),
        ],
        compiler_params=pltpu.CompilerParams(
            collective_id=0, has_side_effects=True, vmem_limit_bytes=48 * 1024 * 1024
        ),
    )(proj_salts, train_lengths, query_lengths, train_acts, train_grads, query_acts, query_grads)


def solution(mesh):
    placed = (
        P("mp", "dp", None, None),
        P("mp", "dp", None, None),
        P("mp", "dp", None, None),
        P("mp", "dp", None, None),
        P("dp"),
        P("dp"),
        P("mp", None),
    )
    return jax.shard_map(shards, mesh=mesh, in_specs=placed, out_specs=P("dp", "mp"), check_vma=False)
```

```python
import functools

import jax
import jax.numpy as jnp
from jax import lax
from jax.experimental import pallas as pl
from jax.experimental.pallas import tpu as pltpu
from jax.sharding import PartitionSpec as P

MESH = pl.DeviceIdType.MESH
R1 = 64
R2 = 64
RIDGE_SCALE = 0.1
LANES = 128
TILE = 8
PLANES = 4
SPOTS = 8
SLICE_ROWS = 4


def sign_table(salt, rows, table_ref):
    half = rows // 2
    row = lax.broadcasted_iota(jnp.int32, (LANES, LANES), 0)
    lane = lax.broadcasted_iota(jnp.int32, (LANES, LANES), 1)
    row = row + jnp.where(lane >= R1, half, 0)
    base = row * 73856093 + (lane & (R1 - 1)) * 19349663 + salt * 83492791
    scale = 1.0 / rows**0.5

    def chunk(step, carry):
        h = base + step * LANES * 73856093
        h = h ^ lax.shift_right_logical(h, 15)
        h = h * 1274126177
        h = h ^ lax.shift_right_logical(h, 13)
        h = h * 668265263
        bit = (lax.shift_right_logical(h, 16) ^ h) & 128
        signs = jnp.where(bit != 0, scale, -scale).astype(jnp.bfloat16)
        table_ref[pl.ds(pl.multiple_of(step * LANES, LANES), LANES), :] = signs
        return carry

    lax.fori_loop(0, half // LANES, chunk, 0, unroll=2)


def projected(tokens, table):
    half = table.shape[0]
    upper = jnp.dot(tokens[:, :half], table, preferred_element_type=jnp.float32)
    lower = jnp.dot(tokens[:, half:], table, preferred_element_type=jnp.float32)
    return upper[:, :R1] + lower[:, R1:]


def rows_by_columns(first, second):
    return lax.dot_general(
        first,
        second,
        (((1,), (1,)), ((), ())),
        precision=lax.Precision.HIGHEST,
        preferred_element_type=jnp.float32,
    )


def features(left, right, length):
    position = lax.broadcasted_iota(jnp.int32, left.shape, 0)
    left = jnp.where(position < length, left, 0.0)
    outer = lax.dot_general(
        left,
        right,
        (((0,), (0,)), ((), ())),
        precision=lax.Precision.HIGHEST,
        preferred_element_type=jnp.float32,
    )
    return jnp.concatenate([outer[: R1 // 2], outer[R1 // 2 :]], axis=1)


def solve(gram, rhs):
    total = gram.shape[0]
    lane = lax.broadcasted_iota(jnp.int32, (TILE, LANES), 1)
    blocks = total // TILE

    def spread(tile, column):
        return jnp.broadcast_to(tile[:, column : column + 1], (TILE, LANES))

    def down(tile, row):
        return jnp.broadcast_to(tile[row : row + 1, :], (TILE, LANES))

    def step(_, tiles):
        pivot, others = tiles[0], tiles[1:]
        columns = [spread(pivot, t) for t in range(TILE)]
        entry = {(k, t): down(columns[t], k) for t in range(TILE) for k in range(t + 1)}
        row = [jnp.where(lane == k, -1.0, jnp.where(lane < TILE, 0.0, down(pivot, k))) for k in range(TILE)]
        for t in range(TILE):
            inverse = 1.0 / entry[t, t]
            row[t] = row[t] * inverse
            scaled = {l: entry[t, l] * inverse for l in range(t + 1, TILE)}
            for k in range(TILE):
                if k == t:
                    continue
                factor = entry[t, k] if k > t else entry[k, t]
                row[k] = row[k] - factor * row[t]
                for l in range(t + 1, TILE):
                    if k < t or l >= k:
                        entry[k, l] = entry[k, l] - factor * scaled[l]
            for l in range(t + 1, TILE):
                entry[t, l] = scaled[l]
        changed = []
        for tile in others:
            terms = [spread(tile, k) * row[k] for k in range(TILE)]
            while len(terms) > 1:
                terms = [a + b for a, b in zip(terms[::2], terms[1::2])]
            tile = jnp.where(lane < TILE, 0.0, tile) - terms[0]
            changed.append(pltpu.roll(tile, LANES - TILE, 1))
        return (*changed[:-1], jnp.zeros_like(pivot), changed[-1])

    tiles = tuple(gram[TILE * b : TILE * (b + 1)] for b in range(blocks)) + (rhs,)
    return lax.fori_loop(0, blocks, step, tiles)[-1]


def kernel(
    salts, train_lengths, query_lengths, train_acts, train_grads, query_acts, query_grads, out_ref,
    acts, grads, table_in, table_out, train_send, query_send, train_recv, query_recv,
    gram_part, cross_part, gram_recv, cross_recv, gram_row, gram_full, score_send, score_recv, result_send, result_recv,
    salts_here, train_lengths_here, query_lengths_here, load_sems, send_sems, recv_sems,
):
    dp, mp = lax.axis_index("dp"), lax.axis_index("mp")
    members, ckpts = lax.axis_size("dp"), lax.axis_size("mp")
    trains, queries = train_acts.shape[1], query_acts.shape[1]
    spot = lax.rem(dp, SPOTS)
    home = dp < SPOTS

    small = [
        pltpu.make_async_copy(salts, salts_here, load_sems.at[4]),
        pltpu.make_async_copy(train_lengths, train_lengths_here, load_sems.at[5]),
        pltpu.make_async_copy(query_lengths, query_lengths_here, load_sems.at[6]),
    ]
    loads = [
        pltpu.make_async_copy(train_grads.at[0], grads.at[pl.ds(0, trains)], load_sems.at[0]),
        pltpu.make_async_copy(query_grads.at[0], grads.at[pl.ds(trains, queries)], load_sems.at[1]),
        pltpu.make_async_copy(train_acts.at[0], acts.at[pl.ds(0, trains)], load_sems.at[2]),
        pltpu.make_async_copy(query_acts.at[0], acts.at[pl.ds(trains, queries)], load_sems.at[3]),
    ]
    for load in small + loads:
        load.start()

    barrier = pltpu.get_barrier_semaphore()

    def greet_dp(peer):
        pl.semaphore_signal(barrier, inc=1, device_id={"dp": peer}, device_id_type=MESH)

    def greet_mp(peer):
        pl.semaphore_signal(barrier, inc=1, device_id={"mp": peer}, device_id_type=MESH)

    def send(phase, source, target, device):
        copy = pltpu.make_async_remote_copy(
            src_ref=source, dst_ref=target, send_sem=send_sems.at[phase], recv_sem=recv_sems.at[phase],
            device_id=device, device_id_type=MESH,
        )
        copy.start()

    def sent(phase, like):
        pltpu.make_async_copy(like, like, send_sems.at[phase]).wait()

    def received(phase, like):
        pltpu.make_async_copy(like, like, recv_sems.at[phase]).wait()

    @pl.when(home)
    def _():
        @pl.loop(1, members)
        def _(k):
            greet_dp(lax.rem(dp + k, members))

        @pl.loop(1, ckpts)
        def _(k):
            greet_mp(lax.rem(mp + k, ckpts))

    @pl.when(jnp.logical_not(home))
    def _():
        @pl.loop(0, SPOTS)
        def _(k):
            greet_dp(k)

    small[0].wait()
    sign_table(salts_here[0, 1], grads.shape[2], table_out)
    sign_table(salts_here[0, 0], acts.shape[2], table_in)

    count, length = acts.shape[0], acts.shape[1]
    loads[0].wait()
    loads[1].wait()
    right = projected(grads[...].reshape(count * length, grads.shape[2]), table_out[...])
    loads[2].wait()
    loads[3].wait()
    left = projected(acts[...].reshape(count * length, acts.shape[2]), table_in[...])
    small[1].wait()
    small[2].wait()
    for e in range(count):
        tokens = slice(e * length, (e + 1) * length)
        tokens_used = train_lengths_here[e] if e < trains else query_lengths_here[e - trains]
        rows = features(left[tokens], right[tokens], tokens_used)
        rows = rows.reshape(SPOTS, SLICE_ROWS, LANES)
        if e < trains:
            for j in range(SLICE_ROWS):
                train_send[:, j // 2, (j % 2) * trains + e, :] = rows[:, j]
        else:
            for j in range(SLICE_ROWS):
                query_send[:, j * queries + e - trains, :] = rows[:, j]

    def spread_features(first):
        @pl.loop(first, SPOTS)
        def _(k):
            to = lax.rem(spot + k, SPOTS)
            send(0, train_send.at[to], train_recv.at[dp], {"dp": to})

        @pl.loop(first, SPOTS)
        def _(k):
            to = lax.rem(spot + k, SPOTS)
            send(1, query_send.at[to], query_recv.at[dp], {"dp": to})

    @pl.when(jnp.logical_not(home))
    def _():
        pl.semaphore_wait(barrier, SPOTS)
        spread_features(0)
        received(6, result_recv)
        out_ref[...] = result_recv[0:queries, 0 : out_ref.shape[1]]
        sent(0, train_send)
        sent(1, query_send)

    @pl.when(home)
    def _():
        pl.semaphore_wait(barrier, members - 1 + ckpts - 1)
        spread_features(1)
        train_recv[dp] = train_send[spot]
        query_recv[dp] = query_send[spot]
        others = pl.ds(0, members - 1)
        received(0, train_recv.at[others])

        low = lax.broadcasted_iota(jnp.int32, (members // 2, TILE, LANES), 1) < trains
        train_rows = []
        for j in range(SLICE_ROWS // 2):
            pairs = train_recv[:, j].reshape(members // 2, 2, TILE, LANES)
            even, odd = pairs[:, 0], pairs[:, 1]
            train_rows.append(jnp.where(low, even, pltpu.roll(odd, trains, 1)))
            train_rows.append(jnp.where(low, pltpu.roll(even, trains, 1), odd))
        train_rows = [rows.reshape(members * trains, LANES) for rows in train_rows]
        gram = rows_by_columns(train_rows[0], train_rows[0])
        for rows in train_rows[1:]:
            gram = gram + rows_by_columns(rows, rows)
        gram_part[...] = gram
        share = members * trains // SPOTS

        @pl.loop(1, SPOTS)
        def _(k):
            to = lax.rem(spot + k, SPOTS)
            send(2, gram_part.at[pl.ds(pl.multiple_of(to * share, share), share)], gram_recv.at[spot], {"dp": to})

        gram_recv[spot] = gram_part[pl.ds(pl.multiple_of(spot * share, share), share), :]

        received(1, query_recv.at[others])
        planes = query_recv[...].reshape(PLANES, SPOTS, TILE, LANES)
        position = lax.broadcasted_iota(jnp.int32, (SPOTS, TILE, LANES), 1) // queries
        cross = None
        for j in range(SLICE_ROWS):
            rows = jnp.zeros((SPOTS, TILE, LANES), jnp.float32)
            for plane in range(PLANES):
                shift = (queries * (plane - j)) % TILE
                moved = pltpu.roll(planes[plane], shift, 1) if shift else planes[plane]
                rows = jnp.where(position == plane, moved, rows)
            term = rows_by_columns(rows.reshape(SPOTS * TILE, LANES), train_rows[j])
            cross = term if cross is None else cross + term
        cross_part[...] = cross.reshape(SPOTS, TILE, LANES)

        @pl.loop(1, SPOTS)
        def _(k):
            to = lax.rem(spot + k, SPOTS)
            send(3, cross_part.at[to], cross_recv.at[spot], {"dp": to})

        cross_recv[spot] = cross_part[spot]

        rest = pl.ds(0, SPOTS - 1)
        received(2, gram_recv.at[rest])
        gram_row[...] = jnp.sum(gram_recv[...], axis=0)
        mine = pl.ds(pl.multiple_of(spot * share, share), share)

        @pl.loop(1, SPOTS)
        def _(k):
            send(4, gram_row, gram_full.at[mine], {"dp": lax.rem(spot + k, SPOTS)})

        gram_full[mine, :] = gram_row[...]
        received(3, cross_recv.at[rest])
        cross_terms = jnp.sum(cross_recv[...], axis=0)
        received(4, gram_full.at[pl.ds(0, share * (SPOTS - 1))])

        gram = gram_full[...]
        total = gram.shape[0]
        diagonal = lax.broadcasted_iota(jnp.int32, gram.shape, 0) == lax.broadcasted_iota(jnp.int32, gram.shape, 1)
        trace = jnp.sum(jnp.where(diagonal, gram, 0.0), axis=(0, 1), keepdims=True)
        ridge = RIDGE_SCALE * trace / total
        system = jnp.where(diagonal, gram + ridge, gram)
        solved = solve(system, cross_terms)

        score_send[...] = solved

        @pl.loop(1, ckpts)
        def _(k):
            send(5, score_send, score_recv.at[mp], {"mp": lax.rem(mp + k, ckpts)})

        score_recv[mp] = solved
        received(5, score_recv.at[pl.ds(0, ckpts - 1)])
        summed = jnp.sum(score_recv[...], axis=0) * (total / ckpts)
        width = out_ref.shape[1]
        summed = pltpu.roll(summed, lax.rem((ckpts - mp) * width, LANES), 1)
        for plane in range(1, PLANES):
            result_send[plane, 0:queries, :] = summed[plane * queries : (plane + 1) * queries]
            result_send[plane, queries:, :] = jnp.zeros((TILE - queries, LANES), jnp.float32)
            send(6, result_send.at[plane], result_recv, {"dp": plane * SPOTS + spot})
        out_ref[...] = summed[0:queries, 0:width]
        sent(0, train_send.at[rest])
        sent(1, query_send.at[rest])
        sent(2, gram_recv.at[rest])
        sent(3, cross_recv.at[rest])
        sent(4, gram_full.at[pl.ds(0, share * (SPOTS - 1))])
        sent(5, score_recv.at[pl.ds(0, ckpts - 1)])
        sent(6, result_send.at[pl.ds(0, PLANES - 1)])


def shards(train_acts, train_grads, query_acts, query_grads, train_lengths, query_lengths, proj_salts):
    _, trains, length, width = train_acts.shape
    queries, out_width = query_acts.shape[1], train_grads.shape[3]
    members, ckpts = lax.axis_size("dp"), lax.axis_size("mp")
    total = trains * members
    f32, bf16 = jnp.float32, jnp.bfloat16
    i32 = jnp.int32
    return pl.pallas_call(
        kernel,
        out_shape=jax.ShapeDtypeStruct((queries, total // ckpts), f32),
        in_specs=[pl.BlockSpec(memory_space=pltpu.HBM)] * 7,
        out_specs=pl.BlockSpec(memory_space=pltpu.VMEM),
        scratch_shapes=[
            pltpu.VMEM((trains + queries, length, width), bf16),
            pltpu.VMEM((trains + queries, length, out_width), bf16),
            pltpu.VMEM((width // 2, LANES), bf16),
            pltpu.VMEM((out_width // 2, LANES), bf16),
            pltpu.VMEM((SPOTS, SLICE_ROWS // 2, TILE, LANES), f32),
            pltpu.VMEM((SPOTS, TILE, LANES), f32),
            pltpu.VMEM((members, SLICE_ROWS // 2, TILE, LANES), f32),
            pltpu.VMEM((members, TILE, LANES), f32),
            pltpu.VMEM((total, LANES), f32),
            pltpu.VMEM((SPOTS, TILE, LANES), f32),
            pltpu.VMEM((SPOTS, total // SPOTS, LANES), f32),
            pltpu.VMEM((SPOTS, TILE, LANES), f32),
            pltpu.VMEM((total // SPOTS, LANES), f32),
            pltpu.VMEM((total, LANES), f32),
            pltpu.VMEM((TILE, LANES), f32),
            pltpu.VMEM((ckpts, TILE, LANES), f32),
            pltpu.VMEM((PLANES, TILE, LANES), f32),
            pltpu.VMEM((TILE, LANES), f32),
            pltpu.SMEM((1, 2), i32),
            pltpu.SMEM((trains,), i32),
            pltpu.SMEM((queries,), i32),
            pltpu.SemaphoreType.DMA((7,)),
            pltpu.SemaphoreType.DMA((7,)),
            pltpu.SemaphoreType.DMA((7,)),
        ],
        compiler_params=pltpu.CompilerParams(
            collective_id=0, has_side_effects=True, vmem_limit_bytes=64 * 1024 * 1024
        ),
    )(proj_salts, train_lengths, query_lengths, train_acts, train_grads, query_acts, query_grads)


def solution(mesh):
    placed = (
        P("mp", "dp", None, None),
        P("mp", "dp", None, None),
        P("mp", "dp", None, None),
        P("mp", "dp", None, None),
        P("dp"),
        P("dp"),
        P("mp", None),
    )
    return jax.shard_map(shards, mesh=mesh, in_specs=placed, out_specs=P("dp", "mp"), check_vma=False)
```

```python
import functools

import jax
import jax.numpy as jnp
from jax import lax
from jax.experimental import pallas as pl
from jax.experimental.pallas import tpu as pltpu
from jax.sharding import PartitionSpec as P

MESH = pl.DeviceIdType.MESH
R1 = 64
R2 = 64
RIDGE_SCALE = 0.1
LANES = 128
TILE = 8
PLANES = 4
SPOTS = 8
PIVOTS = 16
SLICE_ROWS = 4


def sign_table(salt, rows, table_ref):
    half = rows // 2
    row = lax.broadcasted_iota(jnp.int32, (LANES, LANES), 0)
    lane = lax.broadcasted_iota(jnp.int32, (LANES, LANES), 1)
    row = row + jnp.where(lane >= R1, half, 0)
    base = row * 73856093 + (lane & (R1 - 1)) * 19349663 + salt * 83492791
    scale = 1.0 / rows**0.5

    def chunk(step, carry):
        h = base + step * LANES * 73856093
        h = h ^ lax.shift_right_logical(h, 15)
        h = h * 1274126177
        h = h ^ lax.shift_right_logical(h, 13)
        h = h * 668265263
        bit = (lax.shift_right_logical(h, 16) ^ h) & 128
        signs = jnp.where(bit != 0, scale, -scale).astype(jnp.bfloat16)
        table_ref[pl.ds(pl.multiple_of(step * LANES, LANES), LANES), :] = signs
        return carry

    lax.fori_loop(0, half // LANES, chunk, 0, unroll=2)


def projected(tokens, table):
    half = table.shape[0]
    upper = jnp.dot(tokens[:, :half], table, preferred_element_type=jnp.float32)
    lower = jnp.dot(tokens[:, half:], table, preferred_element_type=jnp.float32)
    return upper[:, :R1] + lower[:, R1:]


def rows_by_columns(first, second):
    return lax.dot_general(
        first,
        second,
        (((1,), (1,)), ((), ())),
        precision=lax.Precision.HIGHEST,
        preferred_element_type=jnp.float32,
    )


def features(left, right, length):
    position = lax.broadcasted_iota(jnp.int32, left.shape, 0)
    left = jnp.where(position < length, left, 0.0)
    outer = lax.dot_general(
        left,
        right,
        (((0,), (0,)), ((), ())),
        precision=lax.Precision.HIGHEST,
        preferred_element_type=jnp.float32,
    )
    return jnp.concatenate([outer[: R1 // 2], outer[R1 // 2 :]], axis=1)


def solve(gram, rhs):
    total = gram.shape[0]
    high = PIVOTS // TILE
    sublane = lax.broadcasted_iota(jnp.int32, (TILE, LANES), 0)
    lane = lax.broadcasted_iota(jnp.int32, (TILE, LANES), 1)

    def spread(tile, column):
        return jnp.broadcast_to(tile[:, column : column + 1], (TILE, LANES))

    def down(tile, row):
        return jnp.broadcast_to(tile[row : row + 1, :], (TILE, LANES))

    tiles = [gram[TILE * b : TILE * (b + 1)] for b in range(total // TILE)] + [rhs]
    for start in range(0, total, PIVOTS):
        first = start // TILE
        inside = (lane >= start) & (lane < start + PIVOTS)
        block = tiles[first : first + high]
        columns = [[spread(tile, start + t) for tile in block] for t in range(PIVOTS)]
        rows = [
            jnp.where(inside, jnp.where(lane - start == sublane + TILE * g, -1.0, 0.0), block[g]) for g in range(high)
        ]
        for t in range(PIVOTS):
            g, r = t // TILE, t % TILE
            here = sublane == r
            inverse = 1.0 / down(columns[t][g], r)
            pivot_row = down(rows[g], r) * inverse
            rows = [rows[i] - columns[t][i] * pivot_row for i in range(high)]
            rows[g] = jnp.where(here, pivot_row, rows[g])
            for c in range(t + 1, PIVOTS):
                scaled = down(columns[c][g], r) * inverse
                column = [columns[c][i] - columns[t][i] * scaled for i in range(high)]
                column[g] = jnp.where(here, scaled, column[g])
                columns[c] = column
        pivots = [down(rows[t // TILE], t % TILE) for t in range(PIVOTS)]
        for i in range(first + high, len(tiles)):
            terms = [spread(tiles[i], start + t) * pivots[t] for t in range(PIVOTS)]
            while len(terms) > 1:
                terms = [a + b for a, b in zip(terms[::2], terms[1::2])]
            tiles[i] = jnp.where(inside, 0.0, tiles[i]) - terms[0]
    return tiles[-1]


def kernel(
    salts, train_lengths, query_lengths, train_acts, train_grads, query_acts, query_grads, out_ref,
    acts, grads, table_in, table_out, train_send, query_send, train_recv, query_recv,
    gram_part, cross_part, gram_recv, cross_recv, gram_row, gram_full, score_send, score_recv, result_send, result_recv,
    salts_here, train_lengths_here, query_lengths_here, load_sems, send_sems, recv_sems,
):
    dp, mp = lax.axis_index("dp"), lax.axis_index("mp")
    members, ckpts = lax.axis_size("dp"), lax.axis_size("mp")
    trains, queries = train_acts.shape[1], query_acts.shape[1]
    spot = lax.rem(dp, SPOTS)
    home = dp < SPOTS

    small = [
        pltpu.make_async_copy(salts, salts_here, load_sems.at[4]),
        pltpu.make_async_copy(train_lengths, train_lengths_here, load_sems.at[5]),
        pltpu.make_async_copy(query_lengths, query_lengths_here, load_sems.at[6]),
    ]
    loads = [
        pltpu.make_async_copy(train_grads.at[0], grads.at[pl.ds(0, trains)], load_sems.at[0]),
        pltpu.make_async_copy(query_grads.at[0], grads.at[pl.ds(trains, queries)], load_sems.at[1]),
        pltpu.make_async_copy(train_acts.at[0], acts.at[pl.ds(0, trains)], load_sems.at[2]),
        pltpu.make_async_copy(query_acts.at[0], acts.at[pl.ds(trains, queries)], load_sems.at[3]),
    ]
    for load in small + loads:
        load.start()

    barrier = pltpu.get_barrier_semaphore()

    def greet_dp(peer):
        pl.semaphore_signal(barrier, inc=1, device_id={"dp": peer}, device_id_type=MESH)

    def greet_mp(peer):
        pl.semaphore_signal(barrier, inc=1, device_id={"mp": peer}, device_id_type=MESH)

    def send(phase, source, target, device):
        copy = pltpu.make_async_remote_copy(
            src_ref=source, dst_ref=target, send_sem=send_sems.at[phase], recv_sem=recv_sems.at[phase],
            device_id=device, device_id_type=MESH,
        )
        copy.start()

    def sent(phase, like):
        pltpu.make_async_copy(like, like, send_sems.at[phase]).wait()

    def received(phase, like):
        pltpu.make_async_copy(like, like, recv_sems.at[phase]).wait()

    @pl.when(home)
    def _():
        @pl.loop(1, members)
        def _(k):
            greet_dp(lax.rem(dp + k, members))

        @pl.loop(1, ckpts)
        def _(k):
            greet_mp(lax.rem(mp + k, ckpts))

    @pl.when(jnp.logical_not(home))
    def _():
        @pl.loop(0, SPOTS)
        def _(k):
            greet_dp(k)

    small[0].wait()
    sign_table(salts_here[0, 1], grads.shape[2], table_out)
    sign_table(salts_here[0, 0], acts.shape[2], table_in)

    count, length = acts.shape[0], acts.shape[1]
    loads[0].wait()
    loads[1].wait()
    right = projected(grads[...].reshape(count * length, grads.shape[2]), table_out[...])
    loads[2].wait()
    loads[3].wait()
    left = projected(acts[...].reshape(count * length, acts.shape[2]), table_in[...])
    small[1].wait()
    small[2].wait()
    for e in range(count):
        tokens = slice(e * length, (e + 1) * length)
        tokens_used = train_lengths_here[e] if e < trains else query_lengths_here[e - trains]
        rows = features(left[tokens], right[tokens], tokens_used)
        rows = rows.reshape(SPOTS, SLICE_ROWS, LANES)
        if e < trains:
            for j in range(SLICE_ROWS):
                train_send[:, j // 2, (j % 2) * trains + e, :] = rows[:, j]
        else:
            for j in range(SLICE_ROWS):
                query_send[:, j * queries + e - trains, :] = rows[:, j]

    def spread_features(first):
        @pl.loop(first, SPOTS)
        def _(k):
            to = lax.rem(spot + k, SPOTS)
            send(0, train_send.at[to], train_recv.at[dp], {"dp": to})

        @pl.loop(first, SPOTS)
        def _(k):
            to = lax.rem(spot + k, SPOTS)
            send(1, query_send.at[to], query_recv.at[dp], {"dp": to})

    @pl.when(jnp.logical_not(home))
    def _():
        pl.semaphore_wait(barrier, SPOTS)
        spread_features(0)
        received(6, result_recv)
        out_ref[...] = result_recv[0:queries, 0 : out_ref.shape[1]]
        sent(0, train_send)
        sent(1, query_send)

    @pl.when(home)
    def _():
        pl.semaphore_wait(barrier, members - 1 + ckpts - 1)
        spread_features(1)
        train_recv[dp] = train_send[spot]
        query_recv[dp] = query_send[spot]
        others = pl.ds(0, members - 1)
        received(0, train_recv.at[others])

        low = lax.broadcasted_iota(jnp.int32, (members // 2, TILE, LANES), 1) < trains
        train_rows = []
        for j in range(SLICE_ROWS // 2):
            pairs = train_recv[:, j].reshape(members // 2, 2, TILE, LANES)
            even, odd = pairs[:, 0], pairs[:, 1]
            train_rows.append(jnp.where(low, even, pltpu.roll(odd, trains, 1)))
            train_rows.append(jnp.where(low, pltpu.roll(even, trains, 1), odd))
        train_rows = [rows.reshape(members * trains, LANES) for rows in train_rows]
        gram = rows_by_columns(train_rows[0], train_rows[0])
        for rows in train_rows[1:]:
            gram = gram + rows_by_columns(rows, rows)
        gram_part[...] = gram
        share = members * trains // SPOTS

        @pl.loop(1, SPOTS)
        def _(k):
            to = lax.rem(spot + k, SPOTS)
            send(2, gram_part.at[pl.ds(pl.multiple_of(to * share, share), share)], gram_recv.at[spot], {"dp": to})

        gram_recv[spot] = gram_part[pl.ds(pl.multiple_of(spot * share, share), share), :]

        received(1, query_recv.at[others])
        planes = query_recv[...].reshape(PLANES, SPOTS, TILE, LANES)
        position = lax.broadcasted_iota(jnp.int32, (SPOTS, TILE, LANES), 1) // queries
        cross = None
        for j in range(SLICE_ROWS):
            rows = jnp.zeros((SPOTS, TILE, LANES), jnp.float32)
            for plane in range(PLANES):
                shift = (queries * (plane - j)) % TILE
                moved = pltpu.roll(planes[plane], shift, 1) if shift else planes[plane]
                rows = jnp.where(position == plane, moved, rows)
            term = rows_by_columns(rows.reshape(SPOTS * TILE, LANES), train_rows[j])
            cross = term if cross is None else cross + term
        cross_part[...] = cross.reshape(SPOTS, TILE, LANES)

        @pl.loop(1, SPOTS)
        def _(k):
            to = lax.rem(spot + k, SPOTS)
            send(3, cross_part.at[to], cross_recv.at[spot], {"dp": to})

        cross_recv[spot] = cross_part[spot]

        rest = pl.ds(0, SPOTS - 1)
        received(2, gram_recv.at[rest])
        gram_row[...] = jnp.sum(gram_recv[...], axis=0)
        mine = pl.ds(pl.multiple_of(spot * share, share), share)

        @pl.loop(1, SPOTS)
        def _(k):
            send(4, gram_row, gram_full.at[mine], {"dp": lax.rem(spot + k, SPOTS)})

        gram_full[mine, :] = gram_row[...]
        received(3, cross_recv.at[rest])
        cross_terms = jnp.sum(cross_recv[...], axis=0)
        received(4, gram_full.at[pl.ds(0, share * (SPOTS - 1))])

        gram = gram_full[...]
        total = gram.shape[0]
        diagonal = lax.broadcasted_iota(jnp.int32, gram.shape, 0) == lax.broadcasted_iota(jnp.int32, gram.shape, 1)
        trace = jnp.sum(jnp.where(diagonal, gram, 0.0), axis=(0, 1), keepdims=True)
        ridge = RIDGE_SCALE * trace / total
        system = jnp.where(diagonal, gram + ridge, gram)
        solved = solve(system, cross_terms)

        score_send[...] = solved

        @pl.loop(1, ckpts)
        def _(k):
            send(5, score_send, score_recv.at[mp], {"mp": lax.rem(mp + k, ckpts)})

        score_recv[mp] = solved
        received(5, score_recv.at[pl.ds(0, ckpts - 1)])
        summed = jnp.sum(score_recv[...], axis=0) * (total / ckpts)
        width = out_ref.shape[1]
        summed = pltpu.roll(summed, lax.rem((ckpts - mp) * width, LANES), 1)
        for plane in range(1, PLANES):
            result_send[plane, 0:queries, :] = summed[plane * queries : (plane + 1) * queries]
            result_send[plane, queries:, :] = jnp.zeros((TILE - queries, LANES), jnp.float32)
            send(6, result_send.at[plane], result_recv, {"dp": plane * SPOTS + spot})
        out_ref[...] = summed[0:queries, 0:width]
        sent(0, train_send.at[rest])
        sent(1, query_send.at[rest])
        sent(2, gram_recv.at[rest])
        sent(3, cross_recv.at[rest])
        sent(4, gram_full.at[pl.ds(0, share * (SPOTS - 1))])
        sent(5, score_recv.at[pl.ds(0, ckpts - 1)])
        sent(6, result_send.at[pl.ds(0, PLANES - 1)])


def shards(train_acts, train_grads, query_acts, query_grads, train_lengths, query_lengths, proj_salts):
    _, trains, length, width = train_acts.shape
    queries, out_width = query_acts.shape[1], train_grads.shape[3]
    members, ckpts = lax.axis_size("dp"), lax.axis_size("mp")
    total = trains * members
    f32, bf16 = jnp.float32, jnp.bfloat16
    i32 = jnp.int32
    return pl.pallas_call(
        kernel,
        out_shape=jax.ShapeDtypeStruct((queries, total // ckpts), f32),
        in_specs=[pl.BlockSpec(memory_space=pltpu.HBM)] * 7,
        out_specs=pl.BlockSpec(memory_space=pltpu.VMEM),
        scratch_shapes=[
            pltpu.VMEM((trains + queries, length, width), bf16),
            pltpu.VMEM((trains + queries, length, out_width), bf16),
            pltpu.VMEM((width // 2, LANES), bf16),
            pltpu.VMEM((out_width // 2, LANES), bf16),
            pltpu.VMEM((SPOTS, SLICE_ROWS // 2, TILE, LANES), f32),
            pltpu.VMEM((SPOTS, TILE, LANES), f32),
            pltpu.VMEM((members, SLICE_ROWS // 2, TILE, LANES), f32),
            pltpu.VMEM((members, TILE, LANES), f32),
            pltpu.VMEM((total, LANES), f32),
            pltpu.VMEM((SPOTS, TILE, LANES), f32),
            pltpu.VMEM((SPOTS, total // SPOTS, LANES), f32),
            pltpu.VMEM((SPOTS, TILE, LANES), f32),
            pltpu.VMEM((total // SPOTS, LANES), f32),
            pltpu.VMEM((total, LANES), f32),
            pltpu.VMEM((TILE, LANES), f32),
            pltpu.VMEM((ckpts, TILE, LANES), f32),
            pltpu.VMEM((PLANES, TILE, LANES), f32),
            pltpu.VMEM((TILE, LANES), f32),
            pltpu.SMEM((1, 2), i32),
            pltpu.SMEM((trains,), i32),
            pltpu.SMEM((queries,), i32),
            pltpu.SemaphoreType.DMA((7,)),
            pltpu.SemaphoreType.DMA((7,)),
            pltpu.SemaphoreType.DMA((7,)),
        ],
        compiler_params=pltpu.CompilerParams(
            collective_id=0, has_side_effects=True, vmem_limit_bytes=64 * 1024 * 1024
        ),
    )(proj_salts, train_lengths, query_lengths, train_acts, train_grads, query_acts, query_grads)


def solution(mesh):
    placed = (
        P("mp", "dp", None, None),
        P("mp", "dp", None, None),
        P("mp", "dp", None, None),
        P("mp", "dp", None, None),
        P("dp"),
        P("dp"),
        P("mp", None),
    )
    return jax.shard_map(shards, mesh=mesh, in_specs=placed, out_specs=P("dp", "mp"), check_vma=False)
```

```python
import functools

import jax
import jax.numpy as jnp
from jax import lax
from jax.experimental import pallas as pl
from jax.experimental.pallas import tpu as pltpu
from jax.sharding import PartitionSpec as P

MESH = pl.DeviceIdType.MESH
R1 = 64
R2 = 64
RIDGE_SCALE = 0.1
LANES = 128
TILE = 8
PLANES = 4
FIRST_PLANE = 7
SPOTS = 8
PIVOTS = 16
SLICE_ROWS = 4


def sign_table(salt, rows, table_ref):
    half = rows // 2
    row = lax.broadcasted_iota(jnp.int32, (LANES, LANES), 0)
    lane = lax.broadcasted_iota(jnp.int32, (LANES, LANES), 1)
    row = row + jnp.where(lane >= R1, half, 0)
    base = row * 73856093 + (lane & (R1 - 1)) * 19349663 + salt * 83492791
    scale = 1.0 / rows**0.5

    def chunk(step, carry):
        h = base + step * LANES * 73856093
        h = h ^ lax.shift_right_logical(h, 15)
        h = h * 1274126177
        h = h ^ lax.shift_right_logical(h, 13)
        h = h * 668265263
        bit = (lax.shift_right_logical(h, 16) ^ h) & 128
        signs = jnp.where(bit != 0, scale, -scale).astype(jnp.bfloat16)
        table_ref[pl.ds(pl.multiple_of(step * LANES, LANES), LANES), :] = signs
        return carry

    lax.fori_loop(0, half // LANES, chunk, 0, unroll=2)


def projected(tokens, table):
    half = table.shape[0]
    upper = jnp.dot(tokens[:, :half], table, preferred_element_type=jnp.float32)
    lower = jnp.dot(tokens[:, half:], table, preferred_element_type=jnp.float32)
    return upper[:, :R1] + lower[:, R1:]


def halves(values):
    high = values.astype(jnp.bfloat16)
    return high, (values - high.astype(jnp.float32)).astype(jnp.bfloat16)


def product(first, second, axis):
    (first_high, first_low), (second_high, second_low) = first, second
    return lax.dot_general(
        jnp.concatenate([first_high, first_high, first_low], axis=axis),
        jnp.concatenate([second_high, second_low, second_high], axis=axis),
        (((axis,), (axis,)), ((), ())),
        preferred_element_type=jnp.float32,
    )


def features(left, right, length):
    position = lax.broadcasted_iota(jnp.int32, left.shape, 0)
    left = jnp.where(position < length, left, 0.0)
    outer = product(halves(left), halves(right), 0)
    return jnp.concatenate([outer[: R1 // 2], outer[R1 // 2 :]], axis=1)


def solve(gram, rhs):
    total = gram.shape[0]
    high = PIVOTS // TILE
    sublane = lax.broadcasted_iota(jnp.int32, (TILE, LANES), 0)
    lane = lax.broadcasted_iota(jnp.int32, (TILE, LANES), 1)

    def spread(tile, column):
        return jnp.broadcast_to(tile[:, column : column + 1], (TILE, LANES))

    def down(tile, row):
        return jnp.broadcast_to(tile[row : row + 1, :], (TILE, LANES))

    tiles = [gram[TILE * b : TILE * (b + 1)] for b in range(total // TILE)] + [rhs]
    for start in range(0, total, PIVOTS):
        first = start // TILE
        inside = (lane >= start) & (lane < start + PIVOTS)
        block = tiles[first : first + high]
        columns = [[spread(tile, start + t) for tile in block] for t in range(PIVOTS)]
        rows = [
            jnp.where(inside, jnp.where(lane - start == sublane + TILE * g, -1.0, 0.0), block[g]) for g in range(high)
        ]
        for t in range(PIVOTS):
            g, r = t // TILE, t % TILE
            here = sublane == r
            inverse = 1.0 / down(columns[t][g], r)
            pivot_row = down(rows[g], r) * inverse
            rows = [rows[i] - columns[t][i] * pivot_row for i in range(high)]
            rows[g] = jnp.where(here, pivot_row, rows[g])
            for c in range(t + 1, PIVOTS):
                scaled = down(columns[c][g], r) * inverse
                column = [columns[c][i] - columns[t][i] * scaled for i in range(high)]
                column[g] = jnp.where(here, scaled, column[g])
                columns[c] = column
        pivots = [down(rows[t // TILE], t % TILE) for t in range(PIVOTS)]
        for i in range(first + high, len(tiles)):
            terms = [spread(tiles[i], start + t) * pivots[t] for t in range(PIVOTS)]
            while len(terms) > 1:
                terms = [a + b for a, b in zip(terms[::2], terms[1::2])]
            tiles[i] = jnp.where(inside, 0.0, tiles[i]) - terms[0]
    return tiles[-1]


def kernel(
    salts, train_lengths, query_lengths, train_acts, train_grads, query_acts, query_grads, out_ref,
    acts, grads, table_in, table_out, train_send, query_send, train_recv, query_recv, train_high, train_low,
    gram_part, cross_part, gram_recv, cross_recv, gram_row, gram_full, score_send, score_recv, result_send, result_recv,
    salts_here, train_lengths_here, query_lengths_here, load_sems, send_sems, recv_sems,
):
    dp, mp = lax.axis_index("dp"), lax.axis_index("mp")
    members, ckpts = lax.axis_size("dp"), lax.axis_size("mp")
    trains, queries = train_acts.shape[1], query_acts.shape[1]
    spot = lax.rem(dp, SPOTS)
    home = dp < SPOTS

    small = [
        pltpu.make_async_copy(salts, salts_here, load_sems.at[4]),
        pltpu.make_async_copy(train_lengths, train_lengths_here, load_sems.at[5]),
        pltpu.make_async_copy(query_lengths, query_lengths_here, load_sems.at[6]),
    ]
    loads = [
        pltpu.make_async_copy(train_grads.at[0], grads.at[pl.ds(0, trains)], load_sems.at[0]),
        pltpu.make_async_copy(train_acts.at[0], acts.at[pl.ds(0, trains)], load_sems.at[1]),
        pltpu.make_async_copy(query_grads.at[0], grads.at[pl.ds(trains, queries)], load_sems.at[2]),
        pltpu.make_async_copy(query_acts.at[0], acts.at[pl.ds(trains, queries)], load_sems.at[3]),
    ]
    for load in small + loads[:2]:
        load.start()

    barrier = pltpu.get_barrier_semaphore()

    def greet_dp(peer):
        pl.semaphore_signal(barrier, inc=1, device_id={"dp": peer}, device_id_type=MESH)

    def greet_mp(peer):
        pl.semaphore_signal(barrier, inc=1, device_id={"mp": peer}, device_id_type=MESH)

    def send(phase, source, target, device, arrival=None):
        copy = pltpu.make_async_remote_copy(
            src_ref=source, dst_ref=target, send_sem=send_sems.at[phase],
            recv_sem=recv_sems.at[phase if arrival is None else arrival], device_id=device, device_id_type=MESH,
        )
        copy.start()

    def sent(phase, like):
        pltpu.make_async_copy(like, like, send_sems.at[phase]).wait()

    def received(phase, like):
        pltpu.make_async_copy(like, like, recv_sems.at[phase]).wait()

    @pl.when(home)
    def _():
        @pl.loop(1, members)
        def _(k):
            greet_dp(lax.rem(dp + k, members))

        @pl.loop(1, ckpts)
        def _(k):
            greet_mp(lax.rem(mp + k, ckpts))

    @pl.when(jnp.logical_not(home))
    def _():
        @pl.loop(0, SPOTS)
        def _(k):
            greet_dp(k)

    small[0].wait()
    sign_table(salts_here[0, 1], grads.shape[2], table_out)
    sign_table(salts_here[0, 0], acts.shape[2], table_in)

    length = acts.shape[1]

    def example_features(first, count):
        some = pl.ds(first, count)
        right = projected(grads[some].reshape(count * length, grads.shape[2]), table_out[...])
        loads[1 if first == 0 else 3].wait()
        left = projected(acts[some].reshape(count * length, acts.shape[2]), table_in[...])
        for e in range(count):
            tokens = slice(e * length, (e + 1) * length)
            used = train_lengths_here[e] if first == 0 else query_lengths_here[e]
            yield e, features(left[tokens], right[tokens], used).reshape(SPOTS, SLICE_ROWS, LANES)

    small[1].wait()
    small[2].wait()
    loads[0].wait()
    loads[2].start()
    loads[3].start()
    for e, rows in example_features(0, trains):
        for j in range(SLICE_ROWS):
            train_send[:, j // 2, (j % 2) * trains + e, :] = rows[:, j]

    plane_here = dp // SPOTS

    def send_trains(first):
        @pl.loop(first, SPOTS)
        def _(k):
            to = lax.rem(spot + k, SPOTS)
            send(0, train_send.at[to], train_recv.at[dp], {"dp": to}, arrival=FIRST_PLANE + plane_here)

    def send_queries(first):
        @pl.loop(first, SPOTS)
        def _(k):
            to = lax.rem(spot + k, SPOTS)
            send(1, query_send.at[to], query_recv.at[dp], {"dp": to})

    def query_features():
        loads[2].wait()
        for e, rows in example_features(trains, queries):
            for j in range(SLICE_ROWS):
                query_send[:, j * queries + e, :] = rows[:, j]

    @pl.when(jnp.logical_not(home))
    def _():
        pl.semaphore_wait(barrier, SPOTS)
        send_trains(0)
        query_features()
        sent(0, train_send)
        send_queries(0)
        received(6, result_recv)
        out_ref[...] = result_recv[0:queries, 0 : out_ref.shape[1]]
        sent(1, query_send)

    @pl.when(home)
    def _():
        query_features()
        pl.semaphore_wait(barrier, members - 1 + ckpts - 1)
        send_trains(1)
        send_queries(1)
        train_recv[dp] = train_send[spot]
        query_recv[dp] = query_send[spot]

        low = lax.broadcasted_iota(jnp.int32, (SPOTS // 2, TILE, LANES), 1) < trains
        height = SPOTS * trains
        for plane in (0, 1, 3, 2):
            arrived = SPOTS if plane else SPOTS - 1
            received(FIRST_PLANE + plane, train_recv.at[pl.ds(0, arrived)])
            for j in range(SLICE_ROWS):
                pairs = train_recv[plane * SPOTS : (plane + 1) * SPOTS, j // 2]
                pairs = pairs.reshape(SPOTS // 2, 2, TILE, LANES)
                even, odd = pairs[:, 0], pairs[:, 1]
                if j % 2 == 0:
                    rows = jnp.where(low, even, pltpu.roll(odd, trains, 1))
                else:
                    rows = jnp.where(low, pltpu.roll(even, trains, 1), odd)
                high_part, low_part = halves(rows.reshape(height, LANES))
                train_high[plane * height : (plane + 1) * height, j * LANES : (j + 1) * LANES] = high_part
                train_low[plane * height : (plane + 1) * height, j * LANES : (j + 1) * LANES] = low_part
        train_halves = train_high[...], train_low[...]
        gram_part[...] = product(train_halves, train_halves, 1)
        share = members * trains // SPOTS

        @pl.loop(1, SPOTS)
        def _(k):
            to = lax.rem(spot + k, SPOTS)
            send(2, gram_part.at[pl.ds(pl.multiple_of(to * share, share), share)], gram_recv.at[spot], {"dp": to})

        gram_recv[spot] = gram_part[pl.ds(pl.multiple_of(spot * share, share), share), :]

        rest = pl.ds(0, SPOTS - 1)
        received(2, gram_recv.at[rest])
        gram_row[...] = jnp.sum(gram_recv[...], axis=0)
        mine = pl.ds(pl.multiple_of(spot * share, share), share)

        @pl.loop(1, SPOTS)
        def _(k):
            send(4, gram_row, gram_full.at[mine], {"dp": lax.rem(spot + k, SPOTS)})

        gram_full[mine, :] = gram_row[...]

        received(1, query_recv.at[pl.ds(0, members - 1)])
        planes = query_recv[...].reshape(PLANES, SPOTS, TILE, LANES)
        position = lax.broadcasted_iota(jnp.int32, (SPOTS, TILE, LANES), 1) // queries
        slices = []
        for j in range(SLICE_ROWS):
            rows = jnp.zeros((SPOTS, TILE, LANES), jnp.float32)
            for plane in range(PLANES):
                shift = (queries * (plane - j)) % TILE
                moved = pltpu.roll(planes[plane], shift, 1) if shift else planes[plane]
                rows = jnp.where(position == plane, moved, rows)
            slices.append(rows.reshape(SPOTS * TILE, LANES))
        cross = product(halves(jnp.concatenate(slices, axis=1)), (train_high[...], train_low[...]), 1)
        cross_part[...] = cross.reshape(SPOTS, TILE, LANES)

        @pl.loop(1, SPOTS)
        def _(k):
            to = lax.rem(spot + k, SPOTS)
            send(3, cross_part.at[to], cross_recv.at[spot], {"dp": to})

        cross_recv[spot] = cross_part[spot]

        received(3, cross_recv.at[rest])
        cross_terms = jnp.sum(cross_recv[...], axis=0)
        received(4, gram_full.at[pl.ds(0, share * (SPOTS - 1))])

        gram = gram_full[...]
        total = gram.shape[0]
        diagonal = lax.broadcasted_iota(jnp.int32, gram.shape, 0) == lax.broadcasted_iota(jnp.int32, gram.shape, 1)
        trace = jnp.sum(jnp.where(diagonal, gram, 0.0), axis=(0, 1), keepdims=True)
        ridge = RIDGE_SCALE * trace / total
        system = jnp.where(diagonal, gram + ridge, gram)
        solved = solve(system, cross_terms)

        score_send[...] = solved

        @pl.loop(1, ckpts)
        def _(k):
            send(5, score_send, score_recv.at[mp], {"mp": lax.rem(mp + k, ckpts)})

        score_recv[mp] = solved
        received(5, score_recv.at[pl.ds(0, ckpts - 1)])
        summed = jnp.sum(score_recv[...], axis=0) * (total / ckpts)
        width = out_ref.shape[1]
        summed = pltpu.roll(summed, lax.rem((ckpts - mp) * width, LANES), 1)
        for plane in range(1, PLANES):
            result_send[plane, 0:queries, :] = summed[plane * queries : (plane + 1) * queries]
            result_send[plane, queries:, :] = jnp.zeros((TILE - queries, LANES), jnp.float32)
            send(6, result_send.at[plane], result_recv, {"dp": plane * SPOTS + spot})
        out_ref[...] = summed[0:queries, 0:width]
        sent(0, train_send.at[rest])
        sent(1, query_send.at[rest])
        sent(2, gram_recv.at[rest])
        sent(3, cross_recv.at[rest])
        sent(4, gram_full.at[pl.ds(0, share * (SPOTS - 1))])
        sent(5, score_recv.at[pl.ds(0, ckpts - 1)])
        sent(6, result_send.at[pl.ds(0, PLANES - 1)])


def shards(train_acts, train_grads, query_acts, query_grads, train_lengths, query_lengths, proj_salts):
    _, trains, length, width = train_acts.shape
    queries, out_width = query_acts.shape[1], train_grads.shape[3]
    members, ckpts = lax.axis_size("dp"), lax.axis_size("mp")
    total = trains * members
    f32, bf16 = jnp.float32, jnp.bfloat16
    i32 = jnp.int32
    return pl.pallas_call(
        kernel,
        out_shape=jax.ShapeDtypeStruct((queries, total // ckpts), f32),
        in_specs=[pl.BlockSpec(memory_space=pltpu.HBM)] * 7,
        out_specs=pl.BlockSpec(memory_space=pltpu.VMEM),
        scratch_shapes=[
            pltpu.VMEM((trains + queries, length, width), bf16),
            pltpu.VMEM((trains + queries, length, out_width), bf16),
            pltpu.VMEM((width // 2, LANES), bf16),
            pltpu.VMEM((out_width // 2, LANES), bf16),
            pltpu.VMEM((SPOTS, SLICE_ROWS // 2, TILE, LANES), f32),
            pltpu.VMEM((SPOTS, TILE, LANES), f32),
            pltpu.VMEM((members, SLICE_ROWS // 2, TILE, LANES), f32),
            pltpu.VMEM((members, TILE, LANES), f32),
            pltpu.VMEM((total, SLICE_ROWS * LANES), bf16),
            pltpu.VMEM((total, SLICE_ROWS * LANES), bf16),
            pltpu.VMEM((total, LANES), f32),
            pltpu.VMEM((SPOTS, TILE, LANES), f32),
            pltpu.VMEM((SPOTS, total // SPOTS, LANES), f32),
            pltpu.VMEM((SPOTS, TILE, LANES), f32),
            pltpu.VMEM((total // SPOTS, LANES), f32),
            pltpu.VMEM((total, LANES), f32),
            pltpu.VMEM((TILE, LANES), f32),
            pltpu.VMEM((ckpts, TILE, LANES), f32),
            pltpu.VMEM((PLANES, TILE, LANES), f32),
            pltpu.VMEM((TILE, LANES), f32),
            pltpu.SMEM((1, 2), i32),
            pltpu.SMEM((trains,), i32),
            pltpu.SMEM((queries,), i32),
            pltpu.SemaphoreType.DMA((7,)),
            pltpu.SemaphoreType.DMA((FIRST_PLANE,)),
            pltpu.SemaphoreType.DMA((FIRST_PLANE + PLANES,)),
        ],
        compiler_params=pltpu.CompilerParams(
            collective_id=0, has_side_effects=True, vmem_limit_bytes=64 * 1024 * 1024
        ),
    )(proj_salts, train_lengths, query_lengths, train_acts, train_grads, query_acts, query_grads)


def solution(mesh):
    placed = (
        P("mp", "dp", None, None),
        P("mp", "dp", None, None),
        P("mp", "dp", None, None),
        P("mp", "dp", None, None),
        P("dp"),
        P("dp"),
        P("mp", None),
    )
    return jax.shard_map(shards, mesh=mesh, in_specs=placed, out_specs=P("dp", "mp"), check_vma=False)
```

```python
import functools

import jax
import jax.numpy as jnp
from jax import lax
from jax.experimental import pallas as pl
from jax.experimental.pallas import tpu as pltpu
from jax.sharding import PartitionSpec as P

MESH = pl.DeviceIdType.MESH
R1 = 64
R2 = 64
RIDGE_SCALE = 0.1
LANES = 128
TILE = 8
RING = 4
PLANES = 4
FIRST_PLANE = 7
SPOTS = 8
PIVOTS = 16
LATE = 6
SLICE_ROWS = 4


def sign_table(salt, rows, table_ref):
    half = rows // 2
    row = lax.broadcasted_iota(jnp.int32, (LANES, LANES), 0)
    lane = lax.broadcasted_iota(jnp.int32, (LANES, LANES), 1)
    row = row + jnp.where(lane >= R1, half, 0)
    base = row * 73856093 + (lane & (R1 - 1)) * 19349663 + salt * 83492791
    scale = 1.0 / rows**0.5

    def chunk(step, carry):
        h = base + step * LANES * 73856093
        h = h ^ lax.shift_right_logical(h, 15)
        h = h * 1274126177
        h = h ^ lax.shift_right_logical(h, 13)
        h = h * 668265263
        bit = (lax.shift_right_logical(h, 16) ^ h) & 128
        signs = jnp.where(bit != 0, scale, -scale).astype(jnp.bfloat16)
        table_ref[pl.ds(pl.multiple_of(step * LANES, LANES), LANES), :] = signs
        return carry

    lax.fori_loop(0, half // LANES, chunk, 0, unroll=2)


def projected(tokens, table):
    half = table.shape[0]
    upper = jnp.dot(tokens[:, :half], table, preferred_element_type=jnp.float32)
    lower = jnp.dot(tokens[:, half:], table, preferred_element_type=jnp.float32)
    return upper[:, :R1] + lower[:, R1:]


def halves(values):
    high = values.astype(jnp.bfloat16)
    return high, (values - high.astype(jnp.float32)).astype(jnp.bfloat16)


def product(first, second, axis):
    (first_high, first_low), (second_high, second_low) = first, second
    return lax.dot_general(
        jnp.concatenate([first_high, first_high, first_low], axis=axis),
        jnp.concatenate([second_high, second_low, second_high], axis=axis),
        (((axis,), (axis,)), ((), ())),
        preferred_element_type=jnp.float32,
    )


def features(left, right, length):
    position = lax.broadcasted_iota(jnp.int32, left.shape, 0)
    left = jnp.where(position < length, left, 0.0)
    outer = product(halves(left), halves(right), 0)
    return jnp.concatenate([outer[: R1 // 2], outer[R1 // 2 :]], axis=1)


def solve(gram, late_rhs):
    total = gram.shape[0]
    high = PIVOTS // TILE
    sublane = lax.broadcasted_iota(jnp.int32, (TILE, LANES), 0)
    lane = lax.broadcasted_iota(jnp.int32, (TILE, LANES), 1)

    def spread(tile, column):
        return jnp.broadcast_to(tile[:, column : column + 1], (TILE, LANES))

    def down(tile, row):
        return jnp.broadcast_to(tile[row : row + 1, :], (TILE, LANES))

    def eliminate(tile, start, rows):
        inside = (lane >= start) & (lane < start + PIVOTS)
        terms = [spread(tile, start + t) * down(rows[t // TILE], t % TILE) for t in range(PIVOTS)]
        while len(terms) > 1:
            terms = [a + b for a, b in zip(terms[::2], terms[1::2])]
        return jnp.where(inside, 0.0, tile) - terms[0]

    tiles = [gram[TILE * b : TILE * (b + 1)] for b in range(total // TILE)]
    steps = []
    rhs = None
    for start in range(0, total, PIVOTS):
        if len(steps) == LATE:
            rhs = late_rhs()
            for step in steps:
                rhs = eliminate(rhs, *step)
        first = start // TILE
        inside = (lane >= start) & (lane < start + PIVOTS)
        block = tiles[first : first + high]
        columns = [[spread(tile, start + t) for tile in block] for t in range(PIVOTS)]
        rows = [
            jnp.where(inside, jnp.where(lane - start == sublane + TILE * g, -1.0, 0.0), block[g]) for g in range(high)
        ]
        for t in range(PIVOTS):
            g, r = t // TILE, t % TILE
            here = sublane == r
            inverse = 1.0 / down(columns[t][g], r)
            pivot_row = down(rows[g], r) * inverse
            rows = [rows[i] - columns[t][i] * pivot_row for i in range(high)]
            rows[g] = jnp.where(here, pivot_row, rows[g])
            for c in range(t + 1, PIVOTS):
                scaled = down(columns[c][g], r) * inverse
                column = [columns[c][i] - columns[t][i] * scaled for i in range(high)]
                column[g] = jnp.where(here, scaled, column[g])
                columns[c] = column
        steps.append((start, rows))
        for i in range(first + high, len(tiles)):
            tiles[i] = eliminate(tiles[i], start, rows)
        if rhs is not None:
            rhs = eliminate(rhs, start, rows)
    return rhs


def kernel(
    salts, train_lengths, query_lengths, train_acts, train_grads, query_acts, query_grads, out_ref,
    acts, grads, table_in, table_out, train_send, query_send, train_recv, query_recv, train_high, train_low,
    gram_part, cross_part, gram_recv, cross_recv, gram_row, gram_full, score_send, score_recv, result_send, result_recv,
    salts_here, train_lengths_here, query_lengths_here, load_sems, send_sems, recv_sems,
):
    dp, mp = lax.axis_index("dp"), lax.axis_index("mp")
    members, ckpts = lax.axis_size("dp"), lax.axis_size("mp")
    trains, queries = train_acts.shape[1], query_acts.shape[1]
    spot = lax.rem(dp, SPOTS)
    plane_here, layer_here = dp // SPOTS, mp // RING
    y = lax.rem(mp, RING)
    layers = ckpts // RING
    height = plane_here * layers + layer_here
    home = (height >= 1) & (height <= layers)
    mine = (layer_here + layers - 1) % layers * RING + y
    to_plane, to_layer = (layer_here + 1) // layers, (layer_here + 1) % layers
    in_first = plane_here == 0

    small = [
        pltpu.make_async_copy(salts, salts_here, load_sems.at[4]),
        pltpu.make_async_copy(train_lengths, train_lengths_here, load_sems.at[5]),
        pltpu.make_async_copy(query_lengths, query_lengths_here, load_sems.at[6]),
    ]
    loads = [
        pltpu.make_async_copy(train_grads.at[0], grads.at[pl.ds(0, trains)], load_sems.at[0]),
        pltpu.make_async_copy(train_acts.at[0], acts.at[pl.ds(0, trains)], load_sems.at[1]),
        pltpu.make_async_copy(query_grads.at[0], grads.at[pl.ds(trains, queries)], load_sems.at[2]),
        pltpu.make_async_copy(query_acts.at[0], acts.at[pl.ds(trains, queries)], load_sems.at[3]),
    ]
    for load in small + loads[:2]:
        load.start()

    barrier = pltpu.get_barrier_semaphore()

    def greet(peer):
        pl.semaphore_signal(barrier, inc=1, device_id=peer, device_id_type=MESH)

    def send(phase, source, target, device, arrival=None):
        copy = pltpu.make_async_remote_copy(
            src_ref=source, dst_ref=target, send_sem=send_sems.at[phase],
            recv_sem=recv_sems.at[phase if arrival is None else arrival], device_id=device, device_id_type=MESH,
        )
        copy.start()

    def sent(phase, like):
        pltpu.make_async_copy(like, like, send_sems.at[phase]).wait()

    def received(phase, like):
        pltpu.make_async_copy(like, like, recv_sems.at[phase]).wait()

    @pl.when(home)
    def _():
        @pl.loop(0, members)
        def _(k):
            greet({"dp": k, "mp": mine})

        @pl.loop(1, SPOTS)
        def _(k):
            greet({"dp": plane_here * SPOTS + lax.rem(spot + k, SPOTS), "mp": mp})

    @pl.when(in_first)
    def _():
        @pl.loop(0, ckpts)
        def _(k):
            layer = k // RING + 1

            @pl.when(jnp.logical_not(home) | (k != mine))
            def _():
                greet({"dp": layer // layers * SPOTS + spot, "mp": layer % layers * RING + k % RING})

    @pl.when(jnp.logical_not(in_first))
    def _():
        greet({"dp": spot, "mp": mp})

    small[0].wait()
    sign_table(salts_here[0, 1], grads.shape[2], table_out)
    sign_table(salts_here[0, 0], acts.shape[2], table_in)

    length = acts.shape[1]

    def example_features(first, count):
        some = pl.ds(first, count)
        right = projected(grads[some].reshape(count * length, grads.shape[2]), table_out[...])
        loads[1 if first == 0 else 3].wait()
        left = projected(acts[some].reshape(count * length, acts.shape[2]), table_in[...])
        for e in range(count):
            tokens = slice(e * length, (e + 1) * length)
            used = train_lengths_here[e] if first == 0 else query_lengths_here[e]
            yield e, features(left[tokens], right[tokens], used).reshape(SPOTS, SLICE_ROWS, LANES)

    small[1].wait()
    small[2].wait()
    loads[0].wait()
    loads[2].start()
    loads[3].start()
    for e, rows in example_features(0, trains):
        for j in range(SLICE_ROWS):
            train_send[:, j // 2, (j % 2) * trains + e, :] = rows[:, j]

    homes_wait = SPOTS - 1 + ckpts - in_first.astype(jnp.int32)
    pl.semaphore_wait(barrier, SPOTS + jnp.where(home, homes_wait, 0) + jnp.where(in_first, PLANES - 1, 0))

    @pl.loop(0, SPOTS)
    def _(k):
        to = lax.rem(spot + k, SPOTS)
        there = {"dp": to_plane * SPOTS + to, "mp": to_layer * RING + y}
        send(0, train_send.at[to], train_recv.at[dp], there, arrival=FIRST_PLANE + plane_here)

    loads[2].wait()
    for e, rows in example_features(trains, queries):
        for j in range(SLICE_ROWS):
            query_send[:, j * queries + e, :] = rows[:, j]
    sent(0, train_send)

    @pl.loop(0, SPOTS)
    def _(k):
        to = lax.rem(spot + k, SPOTS)
        send(1, query_send.at[to], query_recv.at[dp], {"dp": to_plane * SPOTS + to, "mp": to_layer * RING + y})

    @pl.when(home)
    def _():
        low = lax.broadcasted_iota(jnp.int32, (SPOTS // 2, TILE, LANES), 1) < trains
        high = SPOTS * trains
        for plane in (0, 1, 3, 2):
            received(FIRST_PLANE + plane, train_recv.at[pl.ds(0, SPOTS)])
            for j in range(SLICE_ROWS):
                pairs = train_recv[plane * SPOTS : (plane + 1) * SPOTS, j // 2]
                pairs = pairs.reshape(SPOTS // 2, 2, TILE, LANES)
                even, odd = pairs[:, 0], pairs[:, 1]
                if j % 2 == 0:
                    rows = jnp.where(low, even, pltpu.roll(odd, trains, 1))
                else:
                    rows = jnp.where(low, pltpu.roll(even, trains, 1), odd)
                high_part, low_part = halves(rows.reshape(high, LANES))
                train_high[plane * high : (plane + 1) * high, j * LANES : (j + 1) * LANES] = high_part
                train_low[plane * high : (plane + 1) * high, j * LANES : (j + 1) * LANES] = low_part
        train_halves = train_high[...], train_low[...]
        gram_part[...] = product(train_halves, train_halves, 1)
        share = members * trains // SPOTS

        def beside(to):
            return {"dp": plane_here * SPOTS + to, "mp": mp}

        @pl.loop(1, SPOTS)
        def _(k):
            to = lax.rem(spot + k, SPOTS)
            send(2, gram_part.at[pl.ds(pl.multiple_of(to * share, share), share)], gram_recv.at[spot], beside(to))

        gram_recv[spot] = gram_part[pl.ds(pl.multiple_of(spot * share, share), share), :]

        rest = pl.ds(0, SPOTS - 1)
        received(2, gram_recv.at[rest])
        gram_row[...] = jnp.sum(gram_recv[...], axis=0)
        my_rows = pl.ds(pl.multiple_of(spot * share, share), share)

        @pl.loop(1, SPOTS)
        def _(k):
            send(4, gram_row, gram_full.at[my_rows], beside(lax.rem(spot + k, SPOTS)))

        gram_full[my_rows, :] = gram_row[...]

        received(1, query_recv)
        planes = query_recv[...].reshape(PLANES, SPOTS, TILE, LANES)
        position = lax.broadcasted_iota(jnp.int32, (SPOTS, TILE, LANES), 1) // queries
        slices = []
        for j in range(SLICE_ROWS):
            rows = jnp.zeros((SPOTS, TILE, LANES), jnp.float32)
            for plane in range(PLANES):
                shift = (queries * (plane - j)) % TILE
                moved = pltpu.roll(planes[plane], shift, 1) if shift else planes[plane]
                rows = jnp.where(position == plane, moved, rows)
            slices.append(rows.reshape(SPOTS * TILE, LANES))
        cross = product(halves(jnp.concatenate(slices, axis=1)), (train_high[...], train_low[...]), 1)
        cross_part[...] = cross.reshape(SPOTS, TILE, LANES)

        @pl.loop(1, SPOTS)
        def _(k):
            to = lax.rem(spot + k, SPOTS)
            send(3, cross_part.at[to], cross_recv.at[spot], beside(to))

        cross_recv[spot] = cross_part[spot]

        received(4, gram_full.at[pl.ds(0, share * (SPOTS - 1))])

        def cross_terms():
            received(3, cross_recv.at[rest])
            return jnp.sum(cross_recv[...], axis=0)

        gram = gram_full[...]
        total = gram.shape[0]
        diagonal = lax.broadcasted_iota(jnp.int32, gram.shape, 0) == lax.broadcasted_iota(jnp.int32, gram.shape, 1)
        trace = jnp.sum(jnp.where(diagonal, gram, 0.0), axis=(0, 1), keepdims=True)
        ridge = RIDGE_SCALE * trace / total
        score_send[...] = solve(jnp.where(diagonal, gram + ridge, gram), cross_terms)

        @pl.loop(0, ckpts)
        def _(k):
            @pl.when(jnp.logical_not(in_first) | (k != mp))
            def _():
                send(5, score_send, score_recv.at[mine], {"dp": spot, "mp": k})

        @pl.when(in_first)
        def _():
            score_recv[mine] = score_send[...]
            sent(5, score_recv.at[pl.ds(0, ckpts - 1)])

        @pl.when(jnp.logical_not(in_first))
        def _():
            sent(5, score_recv)

        sent(2, gram_recv.at[rest])
        sent(3, cross_recv.at[rest])
        sent(4, gram_full.at[pl.ds(0, share * (SPOTS - 1))])

    width = out_ref.shape[1]

    @pl.when(in_first)
    def _():
        @pl.when(home)
        def _():
            received(5, score_recv.at[pl.ds(0, ckpts - 1)])

        @pl.when(jnp.logical_not(home))
        def _():
            received(5, score_recv)

        scale = members * trains / ckpts
        summed = jnp.sum(score_recv[...], axis=0) * scale
        summed = pltpu.roll(summed, lax.rem((ckpts - mp) * width, LANES), 1)
        for plane in range(1, PLANES):
            result_send[plane, 0:queries, :] = summed[plane * queries : (plane + 1) * queries]
            result_send[plane, queries:, :] = jnp.zeros((TILE - queries, LANES), jnp.float32)
            send(6, result_send.at[plane], result_recv, {"dp": plane * SPOTS + spot, "mp": mp})
        out_ref[...] = summed[0:queries, 0:width]
        sent(6, result_send.at[pl.ds(0, PLANES - 1)])

    @pl.when(jnp.logical_not(in_first))
    def _():
        received(6, result_recv)
        out_ref[...] = result_recv[0:queries, 0:width]

    sent(1, query_send)


def shards(train_acts, train_grads, query_acts, query_grads, train_lengths, query_lengths, proj_salts):
    _, trains, length, width = train_acts.shape
    queries, out_width = query_acts.shape[1], train_grads.shape[3]
    members, ckpts = lax.axis_size("dp"), lax.axis_size("mp")
    total = trains * members
    f32, bf16 = jnp.float32, jnp.bfloat16
    i32 = jnp.int32
    return pl.pallas_call(
        kernel,
        out_shape=jax.ShapeDtypeStruct((queries, total // ckpts), f32),
        in_specs=[pl.BlockSpec(memory_space=pltpu.HBM)] * 7,
        out_specs=pl.BlockSpec(memory_space=pltpu.VMEM),
        scratch_shapes=[
            pltpu.VMEM((trains + queries, length, width), bf16),
            pltpu.VMEM((trains + queries, length, out_width), bf16),
            pltpu.VMEM((width // 2, LANES), bf16),
            pltpu.VMEM((out_width // 2, LANES), bf16),
            pltpu.VMEM((SPOTS, SLICE_ROWS // 2, TILE, LANES), f32),
            pltpu.VMEM((SPOTS, TILE, LANES), f32),
            pltpu.VMEM((members, SLICE_ROWS // 2, TILE, LANES), f32),
            pltpu.VMEM((members, TILE, LANES), f32),
            pltpu.VMEM((total, SLICE_ROWS * LANES), bf16),
            pltpu.VMEM((total, SLICE_ROWS * LANES), bf16),
            pltpu.VMEM((total, LANES), f32),
            pltpu.VMEM((SPOTS, TILE, LANES), f32),
            pltpu.VMEM((SPOTS, total // SPOTS, LANES), f32),
            pltpu.VMEM((SPOTS, TILE, LANES), f32),
            pltpu.VMEM((total // SPOTS, LANES), f32),
            pltpu.VMEM((total, LANES), f32),
            pltpu.VMEM((TILE, LANES), f32),
            pltpu.VMEM((ckpts, TILE, LANES), f32),
            pltpu.VMEM((PLANES, TILE, LANES), f32),
            pltpu.VMEM((TILE, LANES), f32),
            pltpu.SMEM((1, 2), i32),
            pltpu.SMEM((trains,), i32),
            pltpu.SMEM((queries,), i32),
            pltpu.SemaphoreType.DMA((7,)),
            pltpu.SemaphoreType.DMA((FIRST_PLANE,)),
            pltpu.SemaphoreType.DMA((FIRST_PLANE + PLANES,)),
        ],
        compiler_params=pltpu.CompilerParams(
            collective_id=0, has_side_effects=True, vmem_limit_bytes=64 * 1024 * 1024
        ),
    )(proj_salts, train_lengths, query_lengths, train_acts, train_grads, query_acts, query_grads)


def solution(mesh):
    placed = (
        P("mp", "dp", None, None),
        P("mp", "dp", None, None),
        P("mp", "dp", None, None),
        P("mp", "dp", None, None),
        P("dp"),
        P("dp"),
        P("mp", None),
    )
    return jax.shard_map(shards, mesh=mesh, in_specs=placed, out_specs=P("dp", "mp"), check_vma=False)
```

```python
import functools

import jax
import jax.numpy as jnp
from jax import lax
from jax.experimental import pallas as pl
from jax.experimental.pallas import tpu as pltpu
from jax.sharding import PartitionSpec as P

MESH = pl.DeviceIdType.MESH
R1 = 64
R2 = 64
RIDGE_SCALE = 0.1
LANES = 128
TILE = 8
RING = 4
PLANES = 4
FIRST_PLANE = 7
SPOTS = 8
PIVOTS = 16
LATE = 6
SLICE_ROWS = 4


def sign_table(salt, rows, table_ref):
    half = rows // 2
    row = lax.broadcasted_iota(jnp.int32, (LANES, LANES), 0)
    lane = lax.broadcasted_iota(jnp.int32, (LANES, LANES), 1)
    row = row + jnp.where(lane >= R1, half, 0)
    base = row * 73856093 + (lane & (R1 - 1)) * 19349663 + salt * 83492791
    scale = 1.0 / rows**0.5

    def chunk(step, carry):
        h = base + step * LANES * 73856093
        h = h ^ lax.shift_right_logical(h, 15)
        h = h * 1274126177
        h = h ^ lax.shift_right_logical(h, 13)
        h = h * 668265263
        bit = (lax.shift_right_logical(h, 16) ^ h) & 128
        signs = jnp.where(bit != 0, scale, -scale).astype(jnp.bfloat16)
        table_ref[pl.ds(pl.multiple_of(step * LANES, LANES), LANES), :] = signs
        return carry

    lax.fori_loop(0, half // LANES, chunk, 0, unroll=2)


def projected(tokens, table):
    half = table.shape[0]
    upper = jnp.dot(tokens[:, :half], table, preferred_element_type=jnp.float32)
    lower = jnp.dot(tokens[:, half:], table, preferred_element_type=jnp.float32)
    return upper[:, :R1] + lower[:, R1:]


def halves(values):
    high = values.astype(jnp.bfloat16)
    return high, (values - high.astype(jnp.float32)).astype(jnp.bfloat16)


def product(first, second, axis):
    (first_high, first_low), (second_high, second_low) = first, second
    return lax.dot_general(
        jnp.concatenate([first_high, first_high, first_low], axis=axis),
        jnp.concatenate([second_high, second_low, second_high], axis=axis),
        (((axis,), (axis,)), ((), ())),
        preferred_element_type=jnp.float32,
    )


def features(left, right, length):
    position = lax.broadcasted_iota(jnp.int32, left.shape, 0)
    left = jnp.where(position < length, left, 0.0)
    outer = product(halves(left), halves(right), 0)
    return jnp.concatenate([outer[: R1 // 2], outer[R1 // 2 :]], axis=1)


def solve(gram, late_rhs):
    total = gram.shape[0]
    high = PIVOTS // TILE
    sublane = lax.broadcasted_iota(jnp.int32, (TILE, LANES), 0)
    lane = lax.broadcasted_iota(jnp.int32, (TILE, LANES), 1)

    def spread(tile, column):
        return jnp.broadcast_to(tile[:, column : column + 1], (TILE, LANES))

    def down(tile, row):
        return jnp.broadcast_to(tile[row : row + 1, :], (TILE, LANES))

    def eliminate(tile, start, rows):
        inside = (lane >= start) & (lane < start + PIVOTS)
        terms = [spread(tile, start + t) * down(rows[t // TILE], t % TILE) for t in range(PIVOTS)]
        while len(terms) > 1:
            terms = [a + b for a, b in zip(terms[::2], terms[1::2])]
        return jnp.where(inside, 0.0, tile) - terms[0]

    tiles = [gram[TILE * b : TILE * (b + 1)] for b in range(total // TILE)]
    steps = []
    rhs = None
    for start in range(0, total, PIVOTS):
        if len(steps) == LATE:
            rhs = late_rhs()
            for step in steps:
                rhs = eliminate(rhs, *step)
        first = start // TILE
        inside = (lane >= start) & (lane < start + PIVOTS)
        block = tiles[first : first + high]
        columns = [[spread(tile, start + t) for tile in block] for t in range(PIVOTS)]
        rows = [
            jnp.where(inside, jnp.where(lane - start == sublane + TILE * g, -1.0, 0.0), block[g]) for g in range(high)
        ]
        for t in range(PIVOTS):
            g, r = t // TILE, t % TILE
            here = sublane == r
            inverse = 1.0 / down(columns[t][g], r)
            pivot_row = down(rows[g], r) * inverse
            rows = [rows[i] - columns[t][i] * pivot_row for i in range(high)]
            rows[g] = jnp.where(here, pivot_row, rows[g])
            for c in range(t + 1, PIVOTS):
                scaled = down(columns[c][g], r) * inverse
                column = [columns[c][i] - columns[t][i] * scaled for i in range(high)]
                column[g] = jnp.where(here, scaled, column[g])
                columns[c] = column
        steps.append((start, rows))
        for i in range(first + high, len(tiles)):
            tiles[i] = eliminate(tiles[i], start, rows)
        if rhs is not None:
            rhs = eliminate(rhs, start, rows)
    return rhs


def kernel(
    salts, train_lengths, query_lengths, train_acts, train_grads, query_acts, query_grads, out_ref,
    acts, grads, table_in, table_out, train_send, query_send, train_recv, query_recv, train_high, train_low,
    gram_part, cross_part, gram_recv, cross_recv, gram_row, gram_full, score_send, score_recv, result_send, result_recv,
    salts_here, train_lengths_here, query_lengths_here, load_sems, send_sems, recv_sems,
):
    dp, mp = lax.axis_index("dp"), lax.axis_index("mp")
    members, ckpts = lax.axis_size("dp"), lax.axis_size("mp")
    trains, queries = train_acts.shape[1], query_acts.shape[1]
    spot = lax.rem(dp, SPOTS)
    plane_here, layer_here = dp // SPOTS, mp // RING
    y = lax.rem(mp, RING)
    layers = ckpts // RING
    home = plane_here == 0
    mine = (layer_here + layers - 1) % layers * RING + y
    home_of_mine = (layer_here + 1) % layers * RING + y

    small = [
        pltpu.make_async_copy(salts, salts_here, load_sems.at[4]),
        pltpu.make_async_copy(train_lengths, train_lengths_here, load_sems.at[5]),
        pltpu.make_async_copy(query_lengths, query_lengths_here, load_sems.at[6]),
    ]
    loads = [
        pltpu.make_async_copy(train_grads.at[0], grads.at[pl.ds(0, trains)], load_sems.at[0]),
        pltpu.make_async_copy(train_acts.at[0], acts.at[pl.ds(0, trains)], load_sems.at[1]),
        pltpu.make_async_copy(query_grads.at[0], grads.at[pl.ds(trains, queries)], load_sems.at[2]),
        pltpu.make_async_copy(query_acts.at[0], acts.at[pl.ds(trains, queries)], load_sems.at[3]),
    ]
    for load in small + loads[:2]:
        load.start()

    barrier = pltpu.get_barrier_semaphore()

    def greet(peer):
        pl.semaphore_signal(barrier, inc=1, device_id=peer, device_id_type=MESH)

    def send(phase, source, target, device, arrival=None):
        copy = pltpu.make_async_remote_copy(
            src_ref=source, dst_ref=target, send_sem=send_sems.at[phase],
            recv_sem=recv_sems.at[phase if arrival is None else arrival], device_id=device, device_id_type=MESH,
        )
        copy.start()

    def sent(phase, like):
        pltpu.make_async_copy(like, like, send_sems.at[phase]).wait()

    def received(phase, like):
        pltpu.make_async_copy(like, like, recv_sems.at[phase]).wait()

    @pl.when(home)
    def _():
        @pl.loop(0, members)
        def _(k):
            greet({"dp": k, "mp": mine})

        @pl.loop(1, SPOTS)
        def _(k):
            greet({"dp": lax.rem(spot + k, SPOTS), "mp": mp})

        @pl.loop(1, ckpts)
        def _(k):
            greet({"dp": dp, "mp": lax.rem(mp + k, ckpts)})

    @pl.when(jnp.logical_not(home))
    def _():
        greet({"dp": spot, "mp": mp})

    small[0].wait()
    sign_table(salts_here[0, 1], grads.shape[2], table_out)
    sign_table(salts_here[0, 0], acts.shape[2], table_in)

    length, width = acts.shape[1], out_ref.shape[1]

    def example_features(first, count):
        some = pl.ds(first, count)
        right = projected(grads[some].reshape(count * length, grads.shape[2]), table_out[...])
        loads[1 if first == 0 else 3].wait()
        left = projected(acts[some].reshape(count * length, acts.shape[2]), table_in[...])
        for e in range(count):
            tokens = slice(e * length, (e + 1) * length)
            used = train_lengths_here[e] if first == 0 else query_lengths_here[e]
            yield e, features(left[tokens], right[tokens], used).reshape(SPOTS, SLICE_ROWS, LANES)

    small[1].wait()
    small[2].wait()
    loads[0].wait()
    loads[2].start()
    loads[3].start()
    for e, rows in example_features(0, trains):
        for j in range(SLICE_ROWS):
            train_send[:, j // 2, (j % 2) * trains + e, :] = rows[:, j]

    pl.semaphore_wait(barrier, SPOTS + jnp.where(home, SPOTS - 1 + ckpts - 1 + PLANES - 1, 0))

    @pl.loop(0, SPOTS)
    def _(k):
        to = lax.rem(spot + k, SPOTS)
        there = {"dp": to, "mp": home_of_mine}
        send(0, train_send.at[to], train_recv.at[dp], there, arrival=FIRST_PLANE + plane_here)

    loads[2].wait()
    for e, rows in example_features(trains, queries):
        for j in range(SLICE_ROWS):
            query_send[:, j * queries + e, :] = rows[:, j]
    sent(0, train_send)

    @pl.loop(0, SPOTS)
    def _(k):
        to = lax.rem(spot + k, SPOTS)
        send(1, query_send.at[to], query_recv.at[dp], {"dp": to, "mp": home_of_mine})

    @pl.when(home)
    def _():
        low = lax.broadcasted_iota(jnp.int32, (SPOTS // 2, TILE, LANES), 1) < trains
        high = SPOTS * trains
        for plane in (0, 1, 3, 2):
            received(FIRST_PLANE + plane, train_recv.at[pl.ds(0, SPOTS)])
            for j in range(SLICE_ROWS):
                pairs = train_recv[plane * SPOTS : (plane + 1) * SPOTS, j // 2]
                pairs = pairs.reshape(SPOTS // 2, 2, TILE, LANES)
                even, odd = pairs[:, 0], pairs[:, 1]
                if j % 2 == 0:
                    rows = jnp.where(low, even, pltpu.roll(odd, trains, 1))
                else:
                    rows = jnp.where(low, pltpu.roll(even, trains, 1), odd)
                high_part, low_part = halves(rows.reshape(high, LANES))
                train_high[plane * high : (plane + 1) * high, j * LANES : (j + 1) * LANES] = high_part
                train_low[plane * high : (plane + 1) * high, j * LANES : (j + 1) * LANES] = low_part
        train_halves = train_high[...], train_low[...]
        gram_part[...] = product(train_halves, train_halves, 1)
        share = members * trains // SPOTS

        def beside(to):
            return {"dp": to, "mp": mp}

        @pl.loop(1, SPOTS)
        def _(k):
            to = lax.rem(spot + k, SPOTS)
            send(2, gram_part.at[pl.ds(pl.multiple_of(to * share, share), share)], gram_recv.at[spot], beside(to))

        gram_recv[spot] = gram_part[pl.ds(pl.multiple_of(spot * share, share), share), :]

        rest = pl.ds(0, SPOTS - 1)
        received(2, gram_recv.at[rest])
        gram_row[...] = jnp.sum(gram_recv[...], axis=0)
        my_rows = pl.ds(pl.multiple_of(spot * share, share), share)

        @pl.loop(1, SPOTS)
        def _(k):
            send(4, gram_row, gram_full.at[my_rows], beside(lax.rem(spot + k, SPOTS)))

        gram_full[my_rows, :] = gram_row[...]

        received(1, query_recv)
        planes = query_recv[...].reshape(PLANES, SPOTS, TILE, LANES)
        position = lax.broadcasted_iota(jnp.int32, (SPOTS, TILE, LANES), 1) // queries
        slices = []
        for j in range(SLICE_ROWS):
            rows = jnp.zeros((SPOTS, TILE, LANES), jnp.float32)
            for plane in range(PLANES):
                shift = (queries * (plane - j)) % TILE
                moved = pltpu.roll(planes[plane], shift, 1) if shift else planes[plane]
                rows = jnp.where(position == plane, moved, rows)
            slices.append(rows.reshape(SPOTS * TILE, LANES))
        cross = product(halves(jnp.concatenate(slices, axis=1)), (train_high[...], train_low[...]), 1)
        cross_part[...] = cross.reshape(SPOTS, TILE, LANES)

        @pl.loop(1, SPOTS)
        def _(k):
            to = lax.rem(spot + k, SPOTS)
            send(3, cross_part.at[to], cross_recv.at[spot], beside(to))

        cross_recv[spot] = cross_part[spot]

        received(4, gram_full.at[pl.ds(0, share * (SPOTS - 1))])

        def cross_terms():
            received(3, cross_recv.at[rest])
            return jnp.sum(cross_recv[...], axis=0)

        gram = gram_full[...]
        total = gram.shape[0]
        diagonal = lax.broadcasted_iota(jnp.int32, gram.shape, 0) == lax.broadcasted_iota(jnp.int32, gram.shape, 1)
        trace = jnp.sum(jnp.where(diagonal, gram, 0.0), axis=(0, 1), keepdims=True)
        ridge = RIDGE_SCALE * trace / total
        score_send[...] = solve(jnp.where(diagonal, gram + ridge, gram), cross_terms)

        @pl.loop(1, ckpts)
        def _(k):
            send(5, score_send, score_recv.at[mine], {"dp": dp, "mp": lax.rem(mp + k, ckpts)})

        score_recv[mine] = score_send[...]
        received(5, score_recv.at[pl.ds(0, ckpts - 1)])
        scale = members * trains / ckpts
        summed = jnp.sum(score_recv[...], axis=0) * scale
        summed = pltpu.roll(summed, lax.rem((ckpts - mp) * width, LANES), 1)
        for plane in range(1, PLANES):
            result_send[plane, 0:queries, :] = summed[plane * queries : (plane + 1) * queries]
            result_send[plane, queries:, :] = jnp.zeros((TILE - queries, LANES), jnp.float32)
            send(6, result_send.at[plane], result_recv, {"dp": plane * SPOTS + spot, "mp": mp})
        out_ref[...] = summed[0:queries, 0:width]
        sent(2, gram_recv.at[rest])
        sent(3, cross_recv.at[rest])
        sent(4, gram_full.at[pl.ds(0, share * (SPOTS - 1))])
        sent(5, score_recv.at[pl.ds(0, ckpts - 1)])
        sent(6, result_send.at[pl.ds(0, PLANES - 1)])

    @pl.when(jnp.logical_not(home))
    def _():
        received(6, result_recv)
        out_ref[...] = result_recv[0:queries, 0:width]

    sent(1, query_send)


def shards(train_acts, train_grads, query_acts, query_grads, train_lengths, query_lengths, proj_salts):
    _, trains, length, width = train_acts.shape
    queries, out_width = query_acts.shape[1], train_grads.shape[3]
    members, ckpts = lax.axis_size("dp"), lax.axis_size("mp")
    total = trains * members
    f32, bf16 = jnp.float32, jnp.bfloat16
    i32 = jnp.int32
    return pl.pallas_call(
        kernel,
        out_shape=jax.ShapeDtypeStruct((queries, total // ckpts), f32),
        in_specs=[pl.BlockSpec(memory_space=pltpu.HBM)] * 7,
        out_specs=pl.BlockSpec(memory_space=pltpu.VMEM),
        scratch_shapes=[
            pltpu.VMEM((trains + queries, length, width), bf16),
            pltpu.VMEM((trains + queries, length, out_width), bf16),
            pltpu.VMEM((width // 2, LANES), bf16),
            pltpu.VMEM((out_width // 2, LANES), bf16),
            pltpu.VMEM((SPOTS, SLICE_ROWS // 2, TILE, LANES), f32),
            pltpu.VMEM((SPOTS, TILE, LANES), f32),
            pltpu.VMEM((members, SLICE_ROWS // 2, TILE, LANES), f32),
            pltpu.VMEM((members, TILE, LANES), f32),
            pltpu.VMEM((total, SLICE_ROWS * LANES), bf16),
            pltpu.VMEM((total, SLICE_ROWS * LANES), bf16),
            pltpu.VMEM((total, LANES), f32),
            pltpu.VMEM((SPOTS, TILE, LANES), f32),
            pltpu.VMEM((SPOTS, total // SPOTS, LANES), f32),
            pltpu.VMEM((SPOTS, TILE, LANES), f32),
            pltpu.VMEM((total // SPOTS, LANES), f32),
            pltpu.VMEM((total, LANES), f32),
            pltpu.VMEM((TILE, LANES), f32),
            pltpu.VMEM((ckpts, TILE, LANES), f32),
            pltpu.VMEM((PLANES, TILE, LANES), f32),
            pltpu.VMEM((TILE, LANES), f32),
            pltpu.SMEM((1, 2), i32),
            pltpu.SMEM((trains,), i32),
            pltpu.SMEM((queries,), i32),
            pltpu.SemaphoreType.DMA((7,)),
            pltpu.SemaphoreType.DMA((FIRST_PLANE,)),
            pltpu.SemaphoreType.DMA((FIRST_PLANE + PLANES,)),
        ],
        compiler_params=pltpu.CompilerParams(
            collective_id=0, has_side_effects=True, vmem_limit_bytes=64 * 1024 * 1024
        ),
    )(proj_salts, train_lengths, query_lengths, train_acts, train_grads, query_acts, query_grads)


def solution(mesh):
    placed = (
        P("mp", "dp", None, None),
        P("mp", "dp", None, None),
        P("mp", "dp", None, None),
        P("mp", "dp", None, None),
        P("dp"),
        P("dp"),
        P("mp", None),
    )
    return jax.shard_map(shards, mesh=mesh, in_specs=placed, out_specs=P("dp", "mp"), check_vma=False)
```

```python
import functools

import jax
import jax.numpy as jnp
from jax import lax
from jax.experimental import pallas as pl
from jax.experimental.pallas import tpu as pltpu
from jax.sharding import PartitionSpec as P

MESH = pl.DeviceIdType.MESH
R1 = 64
R2 = 64
RIDGE_SCALE = 0.1
LANES = 128
TILE = 8
RING = 4
PLANES = 4
QUERY_ROW = 7
SPOTS = 8
CORES = 2
PIVOTS = 16
SLICE_ROWS = 4


def sign_table(salt, rows, table_ref):
    half = rows // 2
    row = lax.broadcasted_iota(jnp.int32, (LANES, LANES), 0)
    lane = lax.broadcasted_iota(jnp.int32, (LANES, LANES), 1)
    row = row + jnp.where(lane >= R1, half, 0)
    base = row * 73856093 + (lane & (R1 - 1)) * 19349663 + salt * 83492791
    scale = 1.0 / rows**0.5

    def chunk(step, carry):
        h = base + step * LANES * 73856093
        h = h ^ lax.shift_right_logical(h, 15)
        h = h * 1274126177
        h = h ^ lax.shift_right_logical(h, 13)
        h = h * 668265263
        bit = (lax.shift_right_logical(h, 16) ^ h) & 128
        signs = jnp.where(bit != 0, scale, -scale).astype(jnp.bfloat16)
        table_ref[pl.ds(pl.multiple_of(step * LANES, LANES), LANES), :] = signs
        return carry

    lax.fori_loop(0, half // LANES, chunk, 0, unroll=2)


def projected(tokens, table):
    half = table.shape[0]
    upper = jnp.dot(tokens[:, :half], table, preferred_element_type=jnp.float32)
    lower = jnp.dot(tokens[:, half:], table, preferred_element_type=jnp.float32)
    return upper[:, :R1] + lower[:, R1:]


def halves(values):
    high = values.astype(jnp.bfloat16)
    return high, (values - high.astype(jnp.float32)).astype(jnp.bfloat16)


def product(first, second, axis):
    (first_high, first_low), (second_high, second_low) = first, second
    return lax.dot_general(
        jnp.concatenate([first_high, first_high, first_low], axis=axis),
        jnp.concatenate([second_high, second_low, second_high], axis=axis),
        (((axis,), (axis,)), ((), ())),
        preferred_element_type=jnp.float32,
    )


def features(left, right, length):
    position = lax.broadcasted_iota(jnp.int32, left.shape, 0)
    left = jnp.where(position < length, left, 0.0)
    outer = product(halves(left), halves(right), 0)
    return jnp.concatenate([outer[: R1 // 2], outer[R1 // 2 :]], axis=1)


def invert(system_ref):
    total = system_ref.shape[0]
    high = PIVOTS // TILE
    sublane = lax.broadcasted_iota(jnp.int32, (TILE, LANES), 0)
    lane = lax.broadcasted_iota(jnp.int32, (TILE, LANES), 1)

    def spread(tile, column):
        return jnp.broadcast_to(tile[:, column : column + 1], (TILE, LANES))

    def down(tile, row):
        return jnp.broadcast_to(tile[row : row + 1, :], (TILE, LANES))

    tiles = [system_ref[TILE * b : TILE * (b + 1), :] for b in range(total // TILE)]
    for start in range(0, total, PIVOTS):
        first = start // TILE
        inside = (lane >= start) & (lane < start + PIVOTS)
        block = tiles[first : first + high]
        columns = [[spread(tile, start + t) for tile in block] for t in range(PIVOTS)]
        rows = [
            jnp.where(inside, jnp.where(lane - start == sublane + TILE * g, -1.0, 0.0), block[g]) for g in range(high)
        ]
        for t in range(PIVOTS):
            g, r = t // TILE, t % TILE
            here = sublane == r
            scale = 1.0 / down(columns[t][g], r)
            pivot_row = down(rows[g], r) * scale
            rows = [rows[i] - columns[t][i] * pivot_row for i in range(high)]
            rows[g] = jnp.where(here, pivot_row, rows[g])
            for c in range(t + 1, PIVOTS):
                scaled = down(columns[c][g], r) * scale
                column = [columns[c][i] - columns[t][i] * scaled for i in range(high)]
                column[g] = jnp.where(here, scaled, column[g])
                columns[c] = column
        pivots = [down(rows[t // TILE], t % TILE) for t in range(PIVOTS)]
        for i in [*range(first + high, len(tiles)), *range(first)]:
            terms = [spread(tiles[i], start + t) * pivots[t] for t in range(PIVOTS)]
            while len(terms) > 1:
                terms = [a + b for a, b in zip(terms[::2], terms[1::2])]
            tiles[i] = jnp.where(inside, 0.0, tiles[i]) - terms[0]
        for g in range(high):
            tiles[first + g] = -rows[g]
    for b, tile in enumerate(tiles):
        system_ref[TILE * b : TILE * (b + 1), :] = tile


def kernel(
    salts, train_lengths, query_lengths, train_acts, train_grads, query_acts, query_grads, out_ref,
    acts, grads, table_in, table_out, train_send, query_send, query_row, train_recv, query_recv, train_high, train_low,
    gram_part, cross_part, gram_recv, cross_recv, gram_row, gram_full, score_send, score_recv, result_send, result_recv,
    salts_here, train_lengths_here, query_lengths_here, load_sems, send_sems, recv_sems, here_sem, go_sem,
):
    dp, mp = lax.axis_index("dp"), lax.axis_index("mp")
    members, ckpts = lax.axis_size("dp"), lax.axis_size("mp")
    trains, queries = train_acts.shape[1], query_acts.shape[1]
    spot = lax.rem(dp, SPOTS)
    plane_here, layer_here = dp // SPOTS, mp // RING
    y = lax.rem(mp, RING)
    layers = ckpts // RING
    home = plane_here == 0
    mine = (layer_here + layers - 1) % layers * RING + y
    last = layers - 1
    late = plane_here == PLANES - 2
    tail_up = (plane_here == PLANES - 1) & (layer_here == last)
    yields_up = (plane_here == PLANES - 1) & (layer_here < last) | late & (layer_here == last)
    tail_down = late & (layer_here == 0)
    yields_down = late & (layer_here > 0) & (layer_here < last)
    tail, yields = tail_up, yields_up
    awaited = jnp.where(tail_up, layers, 0)
    tail_of_mine = {
        "dp": (PLANES - 2 + yields_up.astype(jnp.int32)) * SPOTS + spot,
        "mp": jnp.where(yields_up, last, 0) * RING + y,
    }

    def before(k):
        up = {"plane": PLANES - 1 - k // last, "layer": k}
        down = {"plane": PLANES - 2, "layer": k + 1}
        plane, layer = (jnp.where(tail_up, up[name], down[name]) for name in ("plane", "layer"))
        return {"dp": plane * SPOTS + spot, "mp": layer * RING + y}

    home_of_mine = (layer_here + 1) % layers * RING + y

    small = [
        pltpu.make_async_copy(salts, salts_here, load_sems.at[4]),
        pltpu.make_async_copy(train_lengths, train_lengths_here, load_sems.at[5]),
        pltpu.make_async_copy(query_lengths, query_lengths_here, load_sems.at[6]),
    ]
    loads = [
        pltpu.make_async_copy(train_grads.at[0], grads.at[pl.ds(0, trains)], load_sems.at[0]),
        pltpu.make_async_copy(train_acts.at[0], acts.at[pl.ds(0, trains)], load_sems.at[1]),
        pltpu.make_async_copy(query_grads.at[0], grads.at[pl.ds(trains, queries)], load_sems.at[2]),
        pltpu.make_async_copy(query_acts.at[0], acts.at[pl.ds(trains, queries)], load_sems.at[3]),
    ]
    for load in small + loads[:2]:
        load.start()

    barrier = pltpu.get_barrier_semaphore()

    def greet(peer):
        pl.semaphore_signal(barrier, inc=1, device_id=peer, device_id_type=MESH)

    def send(phase, source, target, device, arrival=None):
        copy = pltpu.make_async_remote_copy(
            src_ref=source, dst_ref=target, send_sem=send_sems.at[phase],
            recv_sem=recv_sems.at[phase if arrival is None else arrival], device_id=device, device_id_type=MESH,
        )
        copy.start()

    def sent(phase, like):
        pltpu.make_async_copy(like, like, send_sems.at[phase]).wait()

    def received(phase, like):
        pltpu.make_async_copy(like, like, recv_sems.at[phase]).wait()

    @pl.when(home)
    def _():
        @pl.loop(0, members)
        def _(k):
            greet({"dp": k, "mp": mine})

        @pl.loop(1, ckpts)
        def _(k):
            greet({"dp": dp, "mp": lax.rem(mp + k, ckpts)})

    @pl.when(jnp.logical_not(home))
    def _():
        greet({"dp": spot, "mp": mp})

    @pl.loop(1, SPOTS)
    def _(k):
        greet({"dp": plane_here * SPOTS + lax.rem(spot + k, SPOTS), "mp": mp})

    @pl.when(tail)
    def _():
        @pl.loop(0, awaited)
        def _(k):
            greet(before(k))

    small[0].wait()
    sign_table(salts_here[0, 1], grads.shape[2], table_out)
    sign_table(salts_here[0, 0], acts.shape[2], table_in)

    length, width = acts.shape[1], out_ref.shape[1]

    def example_features(first, count):
        some = pl.ds(first, count)
        right = projected(grads[some].reshape(count * length, grads.shape[2]), table_out[...])
        loads[1 if first == 0 else 3].wait()
        left = projected(acts[some].reshape(count * length, acts.shape[2]), table_in[...])
        for e in range(count):
            tokens = slice(e * length, (e + 1) * length)
            used = train_lengths_here[e] if first == 0 else query_lengths_here[e]
            yield e, features(left[tokens], right[tokens], used).reshape(SPOTS, SLICE_ROWS, LANES)

    small[1].wait()
    small[2].wait()
    loads[0].wait()
    loads[2].start()
    loads[3].start()
    for e, rows in example_features(0, trains):
        for j in range(SLICE_ROWS):
            train_send[:, j // 2, (j % 2) * trains + e, :] = rows[:, j]

    pl.semaphore_wait(barrier, 2 * SPOTS - 1 + jnp.where(home, ckpts - 1 + PLANES - 1, 0) + yields.astype(jnp.int32))

    @pl.when(yields)
    def _():
        pl.semaphore_signal(here_sem, inc=1, device_id=tail_of_mine, device_id_type=MESH)


    def to_others(action):
        x, core, chips = spot // CORES, lax.rem(spot, CORES), SPOTS // CORES
        for away, other in ((2, 0), (2, 1), (1, 0), (1, 1), (3, 0), (3, 1), (0, 1)):
            to = lax.rem(x + away, chips) * CORES + lax.rem(core + other, CORES)
            action(to, {"dp": plane_here * SPOTS + to, "mp": mp})

    @pl.loop(0, SPOTS)
    def _(k):
        to = lax.rem(spot + k, SPOTS)
        there = {"dp": to, "mp": home_of_mine}
        send(0, train_send.at[to], train_recv.at[dp], there, arrival=QUERY_ROW + 1 + plane_here)

    loads[2].wait()
    for e, rows in example_features(trains, queries):
        for j in range(SLICE_ROWS):
            query_send[:, j * queries + e, :] = rows[:, j]
    to_others(lambda to, device: send(QUERY_ROW, query_send.at[to], query_row.at[spot], device))
    query_row[spot] = query_send[spot]
    received(QUERY_ROW, query_row.at[pl.ds(0, SPOTS - 1)])
    sent(0, train_send)

    @pl.when(tail)
    def _():
        pl.semaphore_wait(here_sem, awaited)

        @pl.loop(0, awaited)
        def _(k):
            pl.semaphore_signal(go_sem, inc=1, device_id=before(k), device_id_type=MESH)

    @pl.when(yields)
    def _():
        pl.semaphore_wait(go_sem, 1)

    in_plane = pl.ds(pl.multiple_of(plane_here * SPOTS, SPOTS), SPOTS)
    send(1, query_row, query_recv.at[in_plane], {"dp": spot, "mp": home_of_mine})

    @pl.when(home)
    def _():
        low = lax.broadcasted_iota(jnp.int32, (SPOTS // 2, TILE, LANES), 1) < trains
        high = SPOTS * trains
        for plane in (0, 1, 3, 2):
            received(QUERY_ROW + 1 + plane, train_recv.at[pl.ds(0, SPOTS)])
            for j in range(SLICE_ROWS):
                pairs = train_recv[plane * SPOTS : (plane + 1) * SPOTS, j // 2]
                pairs = pairs.reshape(SPOTS // 2, 2, TILE, LANES)
                even, odd = pairs[:, 0], pairs[:, 1]
                if j % 2 == 0:
                    rows = jnp.where(low, even, pltpu.roll(odd, trains, 1))
                else:
                    rows = jnp.where(low, pltpu.roll(even, trains, 1), odd)
                high_part, low_part = halves(rows.reshape(high, LANES))
                train_high[plane * high : (plane + 1) * high, j * LANES : (j + 1) * LANES] = high_part
                train_low[plane * high : (plane + 1) * high, j * LANES : (j + 1) * LANES] = low_part
        train_halves = train_high[...], train_low[...]
        gram_part[...] = product(train_halves, train_halves, 1)
        share = members * trains // SPOTS

        def send_part(to, device):
            send(2, gram_part.at[pl.ds(pl.multiple_of(to * share, share), share)], gram_recv.at[spot], device)

        to_others(send_part)

        gram_recv[spot] = gram_part[pl.ds(pl.multiple_of(spot * share, share), share), :]

        rest = pl.ds(0, SPOTS - 1)
        received(2, gram_recv.at[rest])
        gram_row[...] = jnp.sum(gram_recv[...], axis=0)
        my_rows = pl.ds(pl.multiple_of(spot * share, share), share)

        to_others(lambda to, device: send(4, gram_row, gram_full.at[my_rows], device))
        gram_full[my_rows, :] = gram_row[...]

        received(1, query_recv)
        planes = query_recv[...].reshape(PLANES, SPOTS, TILE, LANES)
        position = lax.broadcasted_iota(jnp.int32, (SPOTS, TILE, LANES), 1) // queries
        slices = []
        for j in range(SLICE_ROWS):
            rows = jnp.zeros((SPOTS, TILE, LANES), jnp.float32)
            for plane in range(PLANES):
                shift = (queries * (plane - j)) % TILE
                moved = pltpu.roll(planes[plane], shift, 1) if shift else planes[plane]
                rows = jnp.where(position == plane, moved, rows)
            slices.append(rows.reshape(SPOTS * TILE, LANES))
        cross = product(halves(jnp.concatenate(slices, axis=1)), (train_high[...], train_low[...]), 1)
        cross_part[...] = cross.reshape(SPOTS, TILE, LANES)

        to_others(lambda to, device: send(3, cross_part.at[to], cross_recv.at[spot], device))
        cross_recv[spot] = cross_part[spot]

        received(4, gram_full.at[pl.ds(0, share * (SPOTS - 1))])

        gram = gram_full[...]
        total = gram.shape[0]
        diagonal = lax.broadcasted_iota(jnp.int32, gram.shape, 0) == lax.broadcasted_iota(jnp.int32, gram.shape, 1)
        trace = jnp.sum(jnp.where(diagonal, gram, 0.0), axis=(0, 1), keepdims=True)
        ridge = RIDGE_SCALE * trace / total
        gram_full[...] = jnp.where(diagonal, gram + ridge, gram)
        invert(gram_full)
        received(3, cross_recv.at[rest])
        cross_terms = halves(jnp.sum(cross_recv[...], axis=0))
        score_send[...] = product(cross_terms, halves(gram_full[...]), 1)

        for around in (2, 1, 3, 0):
            for up in (2, 3, 1, 0):
                if around or up:
                    to = lax.rem(layer_here + up, layers) * RING + lax.rem(y + around, RING)
                    send(5, score_send, score_recv.at[mine], {"dp": dp, "mp": to})
        score_recv[mine] = score_send[...]
        received(5, score_recv.at[pl.ds(0, ckpts - 1)])
        scale = members * trains / ckpts
        summed = jnp.sum(score_recv[...], axis=0) * scale
        summed = pltpu.roll(summed, lax.rem((ckpts - mp) * width, LANES), 1)
        for plane in range(1, PLANES):
            result_send[plane, 0:queries, :] = summed[plane * queries : (plane + 1) * queries]
            result_send[plane, queries:, :] = jnp.zeros((TILE - queries, LANES), jnp.float32)
            send(6, result_send.at[plane], result_recv, {"dp": plane * SPOTS + spot, "mp": mp})
        out_ref[...] = summed[0:queries, 0:width]
        sent(2, gram_recv.at[rest])
        sent(3, cross_recv.at[rest])
        sent(4, gram_full.at[pl.ds(0, share * (SPOTS - 1))])
        sent(5, score_recv.at[pl.ds(0, ckpts - 1)])
        sent(6, result_send.at[pl.ds(0, PLANES - 1)])

    @pl.when(jnp.logical_not(home))
    def _():
        received(6, result_recv)
        out_ref[...] = result_recv[0:queries, 0:width]

    sent(1, query_row)
    sent(QUERY_ROW, query_send.at[pl.ds(0, SPOTS - 1)])


def shards(train_acts, train_grads, query_acts, query_grads, train_lengths, query_lengths, proj_salts):
    _, trains, length, width = train_acts.shape
    queries, out_width = query_acts.shape[1], train_grads.shape[3]
    members, ckpts = lax.axis_size("dp"), lax.axis_size("mp")
    total = trains * members
    f32, bf16 = jnp.float32, jnp.bfloat16
    i32 = jnp.int32
    return pl.pallas_call(
        kernel,
        out_shape=jax.ShapeDtypeStruct((queries, total // ckpts), f32),
        in_specs=[pl.BlockSpec(memory_space=pltpu.HBM)] * 7,
        out_specs=pl.BlockSpec(memory_space=pltpu.VMEM),
        scratch_shapes=[
            pltpu.VMEM((trains + queries, length, width), bf16),
            pltpu.VMEM((trains + queries, length, out_width), bf16),
            pltpu.VMEM((width // 2, LANES), bf16),
            pltpu.VMEM((out_width // 2, LANES), bf16),
            pltpu.VMEM((SPOTS, SLICE_ROWS // 2, TILE, LANES), f32),
            pltpu.VMEM((SPOTS, TILE, LANES), f32),
            pltpu.VMEM((SPOTS, TILE, LANES), f32),
            pltpu.VMEM((members, SLICE_ROWS // 2, TILE, LANES), f32),
            pltpu.VMEM((members, TILE, LANES), f32),
            pltpu.VMEM((total, SLICE_ROWS * LANES), bf16),
            pltpu.VMEM((total, SLICE_ROWS * LANES), bf16),
            pltpu.VMEM((total, LANES), f32),
            pltpu.VMEM((SPOTS, TILE, LANES), f32),
            pltpu.VMEM((SPOTS, total // SPOTS, LANES), f32),
            pltpu.VMEM((SPOTS, TILE, LANES), f32),
            pltpu.VMEM((total // SPOTS, LANES), f32),
            pltpu.VMEM((total, LANES), f32),
            pltpu.VMEM((TILE, LANES), f32),
            pltpu.VMEM((ckpts, TILE, LANES), f32),
            pltpu.VMEM((PLANES, TILE, LANES), f32),
            pltpu.VMEM((TILE, LANES), f32),
            pltpu.SMEM((1, 2), i32),
            pltpu.SMEM((trains,), i32),
            pltpu.SMEM((queries,), i32),
            pltpu.SemaphoreType.DMA((7,)),
            pltpu.SemaphoreType.DMA((QUERY_ROW + 1,)),
            pltpu.SemaphoreType.DMA((QUERY_ROW + 1 + PLANES,)),
            pltpu.SemaphoreType.REGULAR,
            pltpu.SemaphoreType.REGULAR,
        ],
        compiler_params=pltpu.CompilerParams(
            collective_id=0, has_side_effects=True, vmem_limit_bytes=64 * 1024 * 1024
        ),
    )(proj_salts, train_lengths, query_lengths, train_acts, train_grads, query_acts, query_grads)


def solution(mesh):
    placed = (
        P("mp", "dp", None, None),
        P("mp", "dp", None, None),
        P("mp", "dp", None, None),
        P("mp", "dp", None, None),
        P("dp"),
        P("dp"),
        P("mp", None),
    )
    return jax.shard_map(shards, mesh=mesh, in_specs=placed, out_specs=P("dp", "mp"), check_vma=False)
```

```python
import functools

import jax
import jax.numpy as jnp
from jax import lax
from jax.experimental import pallas as pl
from jax.experimental.pallas import tpu as pltpu
from jax.sharding import PartitionSpec as P

MESH = pl.DeviceIdType.MESH
R1 = 64
R2 = 64
RIDGE_SCALE = 0.1
LANES = 128
TILE = 8
RING = 4
PLANES = 4
QUERY_ROW = 7
SPOTS = 8
CORES = 2
LATE = 6
PIVOTS = 16
SLICE_ROWS = 4


def sign_table(salt, rows, table_ref):
    half = rows // 2
    row = lax.broadcasted_iota(jnp.int32, (LANES, LANES), 0)
    lane = lax.broadcasted_iota(jnp.int32, (LANES, LANES), 1)
    row = row + jnp.where(lane >= R1, half, 0)
    base = row * 73856093 + (lane & (R1 - 1)) * 19349663 + salt * 83492791
    scale = 1.0 / rows**0.5

    def chunk(step, carry):
        h = base + step * LANES * 73856093
        h = h ^ lax.shift_right_logical(h, 15)
        h = h * 1274126177
        h = h ^ lax.shift_right_logical(h, 13)
        h = h * 668265263
        bit = (lax.shift_right_logical(h, 16) ^ h) & 128
        signs = jnp.where(bit != 0, scale, -scale).astype(jnp.bfloat16)
        table_ref[pl.ds(pl.multiple_of(step * LANES, LANES), LANES), :] = signs
        return carry

    lax.fori_loop(0, half // LANES, chunk, 0, unroll=2)


def projected(tokens, table):
    half = table.shape[0]
    upper = jnp.dot(tokens[:, :half], table, preferred_element_type=jnp.float32)
    lower = jnp.dot(tokens[:, half:], table, preferred_element_type=jnp.float32)
    return upper[:, :R1] + lower[:, R1:]


def halves(values):
    high = values.astype(jnp.bfloat16)
    return high, (values - high.astype(jnp.float32)).astype(jnp.bfloat16)


def product(first, second, axis):
    (first_high, first_low), (second_high, second_low) = first, second
    return lax.dot_general(
        jnp.concatenate([first_high, first_high, first_low], axis=axis),
        jnp.concatenate([second_high, second_low, second_high], axis=axis),
        (((axis,), (axis,)), ((), ())),
        preferred_element_type=jnp.float32,
    )


def features(left, right, length):
    position = lax.broadcasted_iota(jnp.int32, left.shape, 0)
    left = jnp.where(position < length, left, 0.0)
    outer = product(halves(left), halves(right), 0)
    return jnp.concatenate([outer[: R1 // 2], outer[R1 // 2 :]], axis=1)


def solve(system_ref, steps_ref, late_rhs):
    total = system_ref.shape[0]
    high = PIVOTS // TILE
    sublane = lax.broadcasted_iota(jnp.int32, (TILE, LANES), 0)
    lane = lax.broadcasted_iota(jnp.int32, (TILE, LANES), 1)

    def spread(tile, column):
        return jnp.broadcast_to(tile[:, column : column + 1], (TILE, LANES))

    def down(tile, row):
        return jnp.broadcast_to(tile[row : row + 1, :], (TILE, LANES))

    def eliminate(tile, start, rows):
        inside = (lane >= start) & (lane < start + PIVOTS)
        terms = [spread(tile, start + t) * down(rows[t // TILE], t % TILE) for t in range(PIVOTS)]
        while len(terms) > 1:
            terms = [a + b for a, b in zip(terms[::2], terms[1::2])]
        return jnp.where(inside, 0.0, tile) - terms[0]

    def rows_at(ref, first, count):
        return [ref[TILE * b : TILE * (b + 1), :] for b in range(first, first + count)]

    tiles = rows_at(system_ref, 0, total // TILE)
    rhs = None
    for start in range(0, total, PIVOTS):
        first = start // TILE
        if start == LATE * PIVOTS:
            for b in range(first, len(tiles)):
                system_ref[TILE * b : TILE * (b + 1), :] = tiles[b]
            rhs = late_rhs()
            tiles[first:] = rows_at(system_ref, first, len(tiles) - first)
            for done in range(0, start, PIVOTS):
                rhs = eliminate(rhs, done, rows_at(steps_ref, done // TILE, high))
        inside = (lane >= start) & (lane < start + PIVOTS)
        block = tiles[first : first + high]
        columns = [[spread(tile, start + t) for tile in block] for t in range(PIVOTS)]
        rows = [
            jnp.where(inside, jnp.where(lane - start == sublane + TILE * g, -1.0, 0.0), block[g]) for g in range(high)
        ]
        for t in range(PIVOTS):
            g, r = t // TILE, t % TILE
            here = sublane == r
            scale = 1.0 / down(columns[t][g], r)
            pivot_row = down(rows[g], r) * scale
            rows = [rows[i] - columns[t][i] * pivot_row for i in range(high)]
            rows[g] = jnp.where(here, pivot_row, rows[g])
            for c in range(t + 1, PIVOTS):
                scaled = down(columns[c][g], r) * scale
                column = [columns[c][i] - columns[t][i] * scaled for i in range(high)]
                column[g] = jnp.where(here, scaled, column[g])
                columns[c] = column
        for i in range(first + high, len(tiles)):
            tiles[i] = eliminate(tiles[i], start, rows)
        if rhs is not None:
            rhs = eliminate(rhs, start, rows)
        elif start < LATE * PIVOTS:
            for g in range(high):
                steps_ref[TILE * (first + g) : TILE * (first + g + 1), :] = rows[g]
    return rhs


def kernel(
    salts, train_lengths, query_lengths, train_acts, train_grads, query_acts, query_grads, out_ref,
    acts, grads, table_in, table_out, train_send, query_send, query_row, train_recv, query_recv, train_high, train_low,
    gram_part, cross_part, gram_recv, cross_recv, gram_row, gram_full, steps, score_send, score_recv, result_send, result_recv,
    salts_here, train_lengths_here, query_lengths_here, load_sems, send_sems, recv_sems, here_sem, go_sem, reach_sem,
):
    dp, mp = lax.axis_index("dp"), lax.axis_index("mp")
    members, ckpts = lax.axis_size("dp"), lax.axis_size("mp")
    trains, queries = train_acts.shape[1], query_acts.shape[1]
    spot = lax.rem(dp, SPOTS)
    plane_here, layer_here = dp // SPOTS, mp // RING
    y = lax.rem(mp, RING)
    layers = ckpts // RING
    home = plane_here == 0
    mine = (layer_here + layers - 1) % layers * RING + y
    last = layers - 1
    late = plane_here == PLANES - 2
    tail_up = (plane_here == PLANES - 1) & (layer_here == last)
    yields_up = (plane_here == PLANES - 1) & (layer_here < last) | late & (layer_here == last)
    tail_down = late & (layer_here == 0)
    yields_down = late & (layer_here > 0) & (layer_here < last)
    tail, yields = tail_up | tail_down, yields_up | yields_down
    awaited = jnp.where(tail_up, layers, jnp.where(tail_down, layers - 2, 0))
    tail_of_mine = {
        "dp": (PLANES - 2 + yields_up.astype(jnp.int32)) * SPOTS + spot,
        "mp": jnp.where(yields_up, last, 0) * RING + y,
    }

    def before(k):
        up = {"plane": PLANES - 1 - k // last, "layer": k}
        down = {"plane": PLANES - 2, "layer": k + 1}
        plane, layer = (jnp.where(tail_up, up[name], down[name]) for name in ("plane", "layer"))
        return {"dp": plane * SPOTS + spot, "mp": layer * RING + y}

    home_of_mine = (layer_here + 1) % layers * RING + y

    small = [
        pltpu.make_async_copy(salts, salts_here, load_sems.at[4]),
        pltpu.make_async_copy(train_lengths, train_lengths_here, load_sems.at[5]),
        pltpu.make_async_copy(query_lengths, query_lengths_here, load_sems.at[6]),
    ]
    loads = [
        pltpu.make_async_copy(train_grads.at[0], grads.at[pl.ds(0, trains)], load_sems.at[0]),
        pltpu.make_async_copy(train_acts.at[0], acts.at[pl.ds(0, trains)], load_sems.at[1]),
        pltpu.make_async_copy(query_grads.at[0], grads.at[pl.ds(trains, queries)], load_sems.at[2]),
        pltpu.make_async_copy(query_acts.at[0], acts.at[pl.ds(trains, queries)], load_sems.at[3]),
    ]
    for load in small + loads[:2]:
        load.start()

    barrier = pltpu.get_barrier_semaphore()

    def greet(peer):
        pl.semaphore_signal(barrier, inc=1, device_id=peer, device_id_type=MESH)

    def send(phase, source, target, device, arrival=None):
        copy = pltpu.make_async_remote_copy(
            src_ref=source, dst_ref=target, send_sem=send_sems.at[phase],
            recv_sem=recv_sems.at[phase if arrival is None else arrival], device_id=device, device_id_type=MESH,
        )
        copy.start()

    def sent(phase, like):
        pltpu.make_async_copy(like, like, send_sems.at[phase]).wait()

    def received(phase, like):
        pltpu.make_async_copy(like, like, recv_sems.at[phase]).wait()

    @pl.when(home)
    def _():
        @pl.loop(0, members)
        def _(k):
            greet({"dp": k, "mp": mine})

        @pl.loop(1, ckpts)
        def _(k):
            greet({"dp": dp, "mp": lax.rem(mp + k, ckpts)})

        for plane in range(1, PLANES):
            greet({"dp": plane * SPOTS + spot, "mp": mp})

    @pl.loop(1, SPOTS)
    def _(k):
        greet({"dp": plane_here * SPOTS + lax.rem(spot + k, SPOTS), "mp": mp})

    @pl.when(tail)
    def _():
        @pl.loop(0, awaited)
        def _(k):
            greet(before(k))

    small[0].wait()
    sign_table(salts_here[0, 1], grads.shape[2], table_out)
    sign_table(salts_here[0, 0], acts.shape[2], table_in)

    length, width = acts.shape[1], out_ref.shape[1]

    def example_features(first, count):
        some = pl.ds(first, count)
        right = projected(grads[some].reshape(count * length, grads.shape[2]), table_out[...])
        loads[1 if first == 0 else 3].wait()
        left = projected(acts[some].reshape(count * length, acts.shape[2]), table_in[...])
        for e in range(count):
            tokens = slice(e * length, (e + 1) * length)
            used = train_lengths_here[e] if first == 0 else query_lengths_here[e]
            yield e, features(left[tokens], right[tokens], used).reshape(SPOTS, SLICE_ROWS, LANES)

    small[1].wait()
    small[2].wait()
    loads[0].wait()
    loads[2].start()
    loads[3].start()
    for e, rows in example_features(0, trains):
        for j in range(SLICE_ROWS):
            train_send[:, j // 2, (j % 2) * trains + e, :] = rows[:, j]

    pl.semaphore_wait(barrier, 2 * SPOTS - 1 + jnp.where(home, ckpts - 1, 1) + yields.astype(jnp.int32))

    @pl.when(jnp.logical_not(home))
    def _():
        pl.semaphore_signal(reach_sem, inc=1, device_id={"dp": spot, "mp": mp}, device_id_type=MESH)

    @pl.when(yields)
    def _():
        pl.semaphore_signal(here_sem, inc=1, device_id=tail_of_mine, device_id_type=MESH)


    def to_others(action):
        x, core, chips = spot // CORES, lax.rem(spot, CORES), SPOTS // CORES
        for away, other in ((2, 0), (2, 1), (1, 0), (1, 1), (3, 0), (3, 1), (0, 1)):
            to = lax.rem(x + away, chips) * CORES + lax.rem(core + other, CORES)
            action(to, {"dp": plane_here * SPOTS + to, "mp": mp})

    @pl.loop(0, SPOTS)
    def _(k):
        to = lax.rem(spot + k, SPOTS)
        there = {"dp": to, "mp": home_of_mine}
        send(0, train_send.at[to], train_recv.at[dp], there, arrival=QUERY_ROW + 1 + plane_here)

    loads[2].wait()
    for e, rows in example_features(trains, queries):
        for j in range(SLICE_ROWS):
            query_send[:, j * queries + e, :] = rows[:, j]
    to_others(lambda to, device: send(QUERY_ROW, query_send.at[to], query_row.at[spot], device))
    query_row[spot] = query_send[spot]
    received(QUERY_ROW, query_row.at[pl.ds(0, SPOTS - 1)])
    sent(0, train_send)

    @pl.when(tail)
    def _():
        pl.semaphore_wait(here_sem, awaited)

        @pl.loop(0, awaited)
        def _(k):
            pl.semaphore_signal(go_sem, inc=1, device_id=before(k), device_id_type=MESH)

    @pl.when(yields)
    def _():
        pl.semaphore_wait(go_sem, 1)

    in_plane = pl.ds(pl.multiple_of(plane_here * SPOTS, SPOTS), SPOTS)
    send(1, query_row, query_recv.at[in_plane], {"dp": spot, "mp": home_of_mine})

    @pl.when(home)
    def _():
        low = lax.broadcasted_iota(jnp.int32, (SPOTS // 2, TILE, LANES), 1) < trains
        high = SPOTS * trains
        for plane in (0, 1, 3, 2):
            received(QUERY_ROW + 1 + plane, train_recv.at[pl.ds(0, SPOTS)])
            for j in range(SLICE_ROWS):
                pairs = train_recv[plane * SPOTS : (plane + 1) * SPOTS, j // 2]
                pairs = pairs.reshape(SPOTS // 2, 2, TILE, LANES)
                even, odd = pairs[:, 0], pairs[:, 1]
                if j % 2 == 0:
                    rows = jnp.where(low, even, pltpu.roll(odd, trains, 1))
                else:
                    rows = jnp.where(low, pltpu.roll(even, trains, 1), odd)
                high_part, low_part = halves(rows.reshape(high, LANES))
                train_high[plane * high : (plane + 1) * high, j * LANES : (j + 1) * LANES] = high_part
                train_low[plane * high : (plane + 1) * high, j * LANES : (j + 1) * LANES] = low_part
        train_halves = train_high[...], train_low[...]
        gram_part[...] = product(train_halves, train_halves, 1)
        share = members * trains // SPOTS

        def send_part(to, device):
            send(2, gram_part.at[pl.ds(pl.multiple_of(to * share, share), share)], gram_recv.at[spot], device)

        to_others(send_part)

        gram_recv[spot] = gram_part[pl.ds(pl.multiple_of(spot * share, share), share), :]

        rest = pl.ds(0, SPOTS - 1)
        received(2, gram_recv.at[rest])
        gram_row[...] = jnp.sum(gram_recv[...], axis=0)
        my_rows = pl.ds(pl.multiple_of(spot * share, share), share)

        to_others(lambda to, device: send(4, gram_row, gram_full.at[my_rows], device))
        gram_full[my_rows, :] = gram_row[...]

        received(1, query_recv)
        planes = query_recv[...].reshape(PLANES, SPOTS, TILE, LANES)
        position = lax.broadcasted_iota(jnp.int32, (SPOTS, TILE, LANES), 1) // queries
        slices = []
        for j in range(SLICE_ROWS):
            rows = jnp.zeros((SPOTS, TILE, LANES), jnp.float32)
            for plane in range(PLANES):
                shift = (queries * (plane - j)) % TILE
                moved = pltpu.roll(planes[plane], shift, 1) if shift else planes[plane]
                rows = jnp.where(position == plane, moved, rows)
            slices.append(rows.reshape(SPOTS * TILE, LANES))
        cross = product(halves(jnp.concatenate(slices, axis=1)), (train_high[...], train_low[...]), 1)
        cross_part[...] = cross.reshape(SPOTS, TILE, LANES)

        to_others(lambda to, device: send(3, cross_part.at[to], cross_recv.at[spot], device))
        cross_recv[spot] = cross_part[spot]

        received(4, gram_full.at[pl.ds(0, share * (SPOTS - 1))])

        gram = gram_full[...]
        total = gram.shape[0]
        diagonal = lax.broadcasted_iota(jnp.int32, gram.shape, 0) == lax.broadcasted_iota(jnp.int32, gram.shape, 1)
        trace = jnp.sum(jnp.where(diagonal, gram, 0.0), axis=(0, 1), keepdims=True)
        ridge = RIDGE_SCALE * trace / total
        gram_full[...] = jnp.where(diagonal, gram + ridge, gram)

        def cross_terms():
            received(3, cross_recv.at[rest])
            return jnp.sum(cross_recv[...], axis=0)

        score_send[...] = solve(gram_full, steps, cross_terms)

        for around in (2, 1, 3, 0):
            for up in (2, 3, 1, 0):
                if around or up:
                    to = lax.rem(layer_here + up, layers) * RING + lax.rem(y + around, RING)
                    send(5, score_send, score_recv.at[mine], {"dp": dp, "mp": to})
        score_recv[mine] = score_send[...]
        received(5, score_recv.at[pl.ds(0, ckpts - 1)])
        scale = members * trains / ckpts
        summed = jnp.sum(score_recv[...], axis=0) * scale
        summed = pltpu.roll(summed, lax.rem((ckpts - mp) * width, LANES), 1)
        pl.semaphore_wait(reach_sem, PLANES - 1)
        for plane in range(1, PLANES):
            result_send[plane, 0:queries, :] = summed[plane * queries : (plane + 1) * queries]
            result_send[plane, queries:, :] = jnp.zeros((TILE - queries, LANES), jnp.float32)
            send(6, result_send.at[plane], result_recv, {"dp": plane * SPOTS + spot, "mp": mp})
        out_ref[...] = summed[0:queries, 0:width]
        sent(2, gram_recv.at[rest])
        sent(3, cross_recv.at[rest])
        sent(4, gram_full.at[pl.ds(0, share * (SPOTS - 1))])
        sent(5, score_recv.at[pl.ds(0, ckpts - 1)])
        sent(6, result_send.at[pl.ds(0, PLANES - 1)])

    @pl.when(jnp.logical_not(home))
    def _():
        received(6, result_recv)
        out_ref[...] = result_recv[0:queries, 0:width]

    sent(1, query_row)
    sent(QUERY_ROW, query_send.at[pl.ds(0, SPOTS - 1)])


def shards(train_acts, train_grads, query_acts, query_grads, train_lengths, query_lengths, proj_salts):
    _, trains, length, width = train_acts.shape
    queries, out_width = query_acts.shape[1], train_grads.shape[3]
    members, ckpts = lax.axis_size("dp"), lax.axis_size("mp")
    total = trains * members
    f32, bf16 = jnp.float32, jnp.bfloat16
    i32 = jnp.int32
    return pl.pallas_call(
        kernel,
        out_shape=jax.ShapeDtypeStruct((queries, total // ckpts), f32),
        in_specs=[pl.BlockSpec(memory_space=pltpu.HBM)] * 7,
        out_specs=pl.BlockSpec(memory_space=pltpu.VMEM),
        scratch_shapes=[
            pltpu.VMEM((trains + queries, length, width), bf16),
            pltpu.VMEM((trains + queries, length, out_width), bf16),
            pltpu.VMEM((width // 2, LANES), bf16),
            pltpu.VMEM((out_width // 2, LANES), bf16),
            pltpu.VMEM((SPOTS, SLICE_ROWS // 2, TILE, LANES), f32),
            pltpu.VMEM((SPOTS, TILE, LANES), f32),
            pltpu.VMEM((SPOTS, TILE, LANES), f32),
            pltpu.VMEM((members, SLICE_ROWS // 2, TILE, LANES), f32),
            pltpu.VMEM((members, TILE, LANES), f32),
            pltpu.VMEM((total, SLICE_ROWS * LANES), bf16),
            pltpu.VMEM((total, SLICE_ROWS * LANES), bf16),
            pltpu.VMEM((total, LANES), f32),
            pltpu.VMEM((SPOTS, TILE, LANES), f32),
            pltpu.VMEM((SPOTS, total // SPOTS, LANES), f32),
            pltpu.VMEM((SPOTS, TILE, LANES), f32),
            pltpu.VMEM((total // SPOTS, LANES), f32),
            pltpu.VMEM((total, LANES), f32),
            pltpu.VMEM((total, LANES), f32),
            pltpu.VMEM((TILE, LANES), f32),
            pltpu.VMEM((ckpts, TILE, LANES), f32),
            pltpu.VMEM((PLANES, TILE, LANES), f32),
            pltpu.VMEM((TILE, LANES), f32),
            pltpu.SMEM((1, 2), i32),
            pltpu.SMEM((trains,), i32),
            pltpu.SMEM((queries,), i32),
            pltpu.SemaphoreType.DMA((7,)),
            pltpu.SemaphoreType.DMA((QUERY_ROW + 1,)),
            pltpu.SemaphoreType.DMA((QUERY_ROW + 1 + PLANES,)),
            pltpu.SemaphoreType.REGULAR,
            pltpu.SemaphoreType.REGULAR,
            pltpu.SemaphoreType.REGULAR,
        ],
        compiler_params=pltpu.CompilerParams(
            collective_id=0, has_side_effects=True, vmem_limit_bytes=64 * 1024 * 1024
        ),
    )(proj_salts, train_lengths, query_lengths, train_acts, train_grads, query_acts, query_grads)


def solution(mesh):
    placed = (
        P("mp", "dp", None, None),
        P("mp", "dp", None, None),
        P("mp", "dp", None, None),
        P("mp", "dp", None, None),
        P("dp"),
        P("dp"),
        P("mp", None),
    )
    return jax.shard_map(shards, mesh=mesh, in_specs=placed, out_specs=P("dp", "mp"), check_vma=False)
```

```python
import functools

import jax
import jax.numpy as jnp
from jax import lax
from jax.experimental import pallas as pl
from jax.experimental.pallas import tpu as pltpu
from jax.sharding import PartitionSpec as P

MESH = pl.DeviceIdType.MESH
R1 = 64
R2 = 64
RIDGE_SCALE = 0.1
LANES = 128
TILE = 8
RING = 4
PLANES = 4
QUERY_ROW = 7
SPOTS = 8
CORES = 2
LATE = 6
PIVOTS = 16
SLICE_ROWS = 4


def sign_table(salt, rows, table_ref):
    half = rows // 2
    row = lax.broadcasted_iota(jnp.int32, (LANES, LANES), 0)
    lane = lax.broadcasted_iota(jnp.int32, (LANES, LANES), 1)
    row = row + jnp.where(lane >= R1, half, 0)
    base = row * 73856093 + (lane & (R1 - 1)) * 19349663 + salt * 83492791
    scale = 1.0 / rows**0.5

    def chunk(step, carry):
        h = base + step * LANES * 73856093
        h = h ^ lax.shift_right_logical(h, 15)
        h = h * 1274126177
        h = h ^ lax.shift_right_logical(h, 13)
        h = h * 668265263
        bit = (lax.shift_right_logical(h, 16) ^ h) & 128
        signs = jnp.where(bit != 0, scale, -scale).astype(jnp.bfloat16)
        table_ref[pl.ds(pl.multiple_of(step * LANES, LANES), LANES), :] = signs
        return carry

    lax.fori_loop(0, half // LANES, chunk, 0, unroll=2)


def projected(tokens, table):
    half = table.shape[0]
    upper = jnp.dot(tokens[:, :half], table, preferred_element_type=jnp.float32)
    lower = jnp.dot(tokens[:, half:], table, preferred_element_type=jnp.float32)
    return upper[:, :R1] + lower[:, R1:]


def halves(values):
    high = values.astype(jnp.bfloat16)
    return high, (values - high.astype(jnp.float32)).astype(jnp.bfloat16)


def product(first, second, axis):
    (first_high, first_low), (second_high, second_low) = first, second
    return lax.dot_general(
        jnp.concatenate([first_high, first_high, first_low], axis=axis),
        jnp.concatenate([second_high, second_low, second_high], axis=axis),
        (((axis,), (axis,)), ((), ())),
        preferred_element_type=jnp.float32,
    )


def features(left, right, length):
    position = lax.broadcasted_iota(jnp.int32, left.shape, 0)
    left = jnp.where(position < length, left, 0.0)
    outer = product(halves(left), halves(right), 0)
    return jnp.concatenate([outer[: R1 // 2], outer[R1 // 2 :]], axis=1)


def solve(system_ref, steps_ref, late_rhs):
    total = system_ref.shape[0]
    high = PIVOTS // TILE
    sublane = lax.broadcasted_iota(jnp.int32, (TILE, LANES), 0)
    lane = lax.broadcasted_iota(jnp.int32, (TILE, LANES), 1)

    def spread(tile, column):
        return jnp.broadcast_to(tile[:, column : column + 1], (TILE, LANES))

    def down(tile, row):
        return jnp.broadcast_to(tile[row : row + 1, :], (TILE, LANES))

    def eliminate(tile, start, rows):
        inside = (lane >= start) & (lane < start + PIVOTS)
        terms = [spread(tile, start + t) * down(rows[t // TILE], t % TILE) for t in range(PIVOTS)]
        while len(terms) > 1:
            terms = [a + b for a, b in zip(terms[::2], terms[1::2])]
        return jnp.where(inside, 0.0, tile) - terms[0]

    def rows_at(ref, first, count):
        return [ref[TILE * b : TILE * (b + 1), :] for b in range(first, first + count)]

    tiles = rows_at(system_ref, 0, total // TILE)
    rhs = None
    for start in range(0, total, PIVOTS):
        first = start // TILE
        if start == LATE * PIVOTS:
            for b in range(first, len(tiles)):
                system_ref[TILE * b : TILE * (b + 1), :] = tiles[b]
            rhs = late_rhs()
            tiles[first:] = rows_at(system_ref, first, len(tiles) - first)
            for done in range(0, start, PIVOTS):
                rhs = eliminate(rhs, done, rows_at(steps_ref, done // TILE, high))
        inside = (lane >= start) & (lane < start + PIVOTS)
        block = tiles[first : first + high]
        columns = [[spread(tile, start + t) for tile in block] for t in range(PIVOTS)]
        rows = [
            jnp.where(inside, jnp.where(lane - start == sublane + TILE * g, -1.0, 0.0), block[g]) for g in range(high)
        ]
        for t in range(PIVOTS):
            g, r = t // TILE, t % TILE
            here = sublane == r
            scale = 1.0 / down(columns[t][g], r)
            pivot_row = down(rows[g], r) * scale
            rows = [rows[i] - columns[t][i] * pivot_row for i in range(high)]
            rows[g] = jnp.where(here, pivot_row, rows[g])
            for c in range(t + 1, PIVOTS):
                scaled = down(columns[c][g], r) * scale
                column = [columns[c][i] - columns[t][i] * scaled for i in range(high)]
                column[g] = jnp.where(here, scaled, column[g])
                columns[c] = column
        for i in range(first + high, len(tiles)):
            tiles[i] = eliminate(tiles[i], start, rows)
        if rhs is not None:
            rhs = eliminate(rhs, start, rows)
        elif start < LATE * PIVOTS:
            for g in range(high):
                steps_ref[TILE * (first + g) : TILE * (first + g + 1), :] = rows[g]
    return rhs


def kernel(
    salts, train_lengths, query_lengths, train_acts, train_grads, query_acts, query_grads, out_ref,
    acts, grads, table_in, table_out, train_send, query_send, query_row, train_recv, query_recv, train_high, train_low,
    gram_part, cross_part, gram_recv, cross_recv, gram_row, gram_full, steps, score_send, score_recv, result_send, result_recv,
    out_here, projections, salts_here, train_lengths_here, query_lengths_here, load_sems, send_sems, recv_sems, here_sem, go_sem, reach_sem,
):
    dp, mp = lax.axis_index("dp"), lax.axis_index("mp")
    members, ckpts = lax.axis_size("dp"), lax.axis_size("mp")
    trains, queries = train_acts.shape[1], query_acts.shape[1]
    spot = lax.rem(dp, SPOTS)
    plane_here, layer_here = dp // SPOTS, mp // RING
    y = lax.rem(mp, RING)
    layers = ckpts // RING
    home = plane_here == 0
    mine = (layer_here + layers - 1) % layers * RING + y
    last = layers - 1
    late = plane_here == PLANES - 2
    tail_up = (plane_here == PLANES - 1) & (layer_here == last)
    yields_up = (plane_here == PLANES - 1) & (layer_here < last) | late & (layer_here == last)
    tail_down = late & (layer_here == 0)
    yields_down = late & (layer_here > 0) & (layer_here < last)
    tail, yields = tail_up | tail_down, yields_up | yields_down
    awaited = jnp.where(tail_up, layers, jnp.where(tail_down, layers - 2, 0))
    tail_of_mine = {
        "dp": (PLANES - 2 + yields_up.astype(jnp.int32)) * SPOTS + spot,
        "mp": jnp.where(yields_up, last, 0) * RING + y,
    }

    def before(k):
        up = {"plane": PLANES - 1 - k // last, "layer": k}
        down = {"plane": PLANES - 2, "layer": k + 1}
        plane, layer = (jnp.where(tail_up, up[name], down[name]) for name in ("plane", "layer"))
        return {"dp": plane * SPOTS + spot, "mp": layer * RING + y}

    home_of_mine = (layer_here + 1) % layers * RING + y

    half = acts.shape[2] // 2
    first_half, second_half = pl.ds(0, half), pl.ds(half, half)
    small = [
        pltpu.make_async_copy(salts, salts_here, load_sems.at[4]),
        pltpu.make_async_copy(train_lengths, train_lengths_here, load_sems.at[5]),
        pltpu.make_async_copy(query_lengths, query_lengths_here, load_sems.at[6]),
    ]
    loads = [
        pltpu.make_async_copy(train_grads.at[0], grads.at[pl.ds(0, trains)], load_sems.at[0]),
        pltpu.make_async_copy(train_acts.at[0, :, :, first_half], acts.at[pl.ds(0, trains), :, first_half], load_sems.at[1]),
        pltpu.make_async_copy(query_grads.at[0], grads.at[pl.ds(trains, queries)], load_sems.at[2]),
        pltpu.make_async_copy(query_acts.at[0], acts.at[pl.ds(trains, queries)], load_sems.at[3]),
        pltpu.make_async_copy(train_acts.at[0, :, :, second_half], acts.at[pl.ds(0, trains), :, second_half], load_sems.at[7]),
    ]
    for load in [*small, *loads[:2], loads[4]]:
        load.start()

    barrier = pltpu.get_barrier_semaphore()

    def greet(peer):
        pl.semaphore_signal(barrier, inc=1, device_id=peer, device_id_type=MESH)

    def send(phase, source, target, device, arrival=None):
        copy = pltpu.make_async_remote_copy(
            src_ref=source, dst_ref=target, send_sem=send_sems.at[phase],
            recv_sem=recv_sems.at[phase if arrival is None else arrival], device_id=device, device_id_type=MESH,
        )
        copy.start()

    def sent(phase, like):
        pltpu.make_async_copy(like, like, send_sems.at[phase]).wait()

    def received(phase, like):
        pltpu.make_async_copy(like, like, recv_sems.at[phase]).wait()

    @pl.when(home)
    def _():
        @pl.loop(0, members)
        def _(k):
            greet({"dp": k, "mp": mine})

        @pl.loop(1, ckpts)
        def _(k):
            greet({"dp": dp, "mp": lax.rem(mp + k, ckpts)})

        for plane in range(1, PLANES):
            greet({"dp": plane * SPOTS + spot, "mp": mp})

    @pl.loop(1, SPOTS)
    def _(k):
        greet({"dp": plane_here * SPOTS + lax.rem(spot + k, SPOTS), "mp": mp})

    @pl.when(tail)
    def _():
        @pl.loop(0, awaited)
        def _(k):
            greet(before(k))

    small[0].wait()
    sign_table(salts_here[0, 1], grads.shape[2], table_out)
    sign_table(salts_here[0, 0], acts.shape[2], table_in)

    length, width = acts.shape[1], out_ref.shape[1]
    write = pltpu.make_async_copy(out_here, out_ref, load_sems.at[8])

    def example_features(first, count):
        some = pl.ds(first, count)
        right = projected(grads[some].reshape(count * length, grads.shape[2]), table_out[...])
        if first == 0:
            projections[0, :, 0:R2] = right
            loads[1].wait()
            tokens = acts[some, :, first_half].reshape(count * length, half)
            projections[1] = jnp.dot(tokens, table_in[...], preferred_element_type=jnp.float32)
            loads[4].wait()
            tokens = acts[some, :, second_half].reshape(count * length, half)
            left = jnp.dot(tokens, table_in[...], preferred_element_type=jnp.float32)
            left = projections[1, :, 0:R1] + left[:, R1:]
            right = projections[0, :, 0:R2]
        else:
            loads[3].wait()
            left = projected(acts[some].reshape(count * length, acts.shape[2]), table_in[...])
        for e in range(count):
            tokens = slice(e * length, (e + 1) * length)
            used = train_lengths_here[e] if first == 0 else query_lengths_here[e]
            yield e, features(left[tokens], right[tokens], used).reshape(SPOTS, SLICE_ROWS, LANES)

    small[1].wait()
    small[2].wait()
    loads[0].wait()
    loads[2].start()
    loads[3].start()
    for e, rows in example_features(0, trains):
        for j in range(SLICE_ROWS):
            train_send[:, j // 2, (j % 2) * trains + e, :] = rows[:, j]

    pl.semaphore_wait(barrier, 2 * SPOTS - 1 + jnp.where(home, ckpts - 1, 1) + yields.astype(jnp.int32))

    @pl.when(jnp.logical_not(home))
    def _():
        pl.semaphore_signal(reach_sem, inc=1, device_id={"dp": spot, "mp": mp}, device_id_type=MESH)

    @pl.when(yields)
    def _():
        pl.semaphore_signal(here_sem, inc=1, device_id=tail_of_mine, device_id_type=MESH)


    def to_others(action):
        x, core, chips = spot // CORES, lax.rem(spot, CORES), SPOTS // CORES
        for away, other in ((2, 0), (2, 1), (1, 0), (1, 1), (3, 0), (3, 1), (0, 1)):
            to = lax.rem(x + away, chips) * CORES + lax.rem(core + other, CORES)
            action(to, {"dp": plane_here * SPOTS + to, "mp": mp})

    @pl.loop(0, SPOTS)
    def _(k):
        to = lax.rem(spot + k, SPOTS)
        there = {"dp": to, "mp": home_of_mine}
        send(0, train_send.at[to], train_recv.at[dp], there, arrival=QUERY_ROW + 1 + plane_here)

    loads[2].wait()
    for e, rows in example_features(trains, queries):
        for j in range(SLICE_ROWS):
            query_send[:, j * queries + e, :] = rows[:, j]
    to_others(lambda to, device: send(QUERY_ROW, query_send.at[to], query_row.at[spot], device))
    query_row[spot] = query_send[spot]
    received(QUERY_ROW, query_row.at[pl.ds(0, SPOTS - 1)])
    sent(0, train_send)

    @pl.when(tail)
    def _():
        pl.semaphore_wait(here_sem, awaited)

        @pl.loop(0, awaited)
        def _(k):
            pl.semaphore_signal(go_sem, inc=1, device_id=before(k), device_id_type=MESH)

    @pl.when(yields)
    def _():
        pl.semaphore_wait(go_sem, 1)

    in_plane = pl.ds(pl.multiple_of(plane_here * SPOTS, SPOTS), SPOTS)
    send(1, query_row, query_recv.at[in_plane], {"dp": spot, "mp": home_of_mine})

    @pl.when(home)
    def _():
        low = lax.broadcasted_iota(jnp.int32, (SPOTS // 2, TILE, LANES), 1) < trains
        high = SPOTS * trains
        for plane in (0, 1, 3, 2):
            received(QUERY_ROW + 1 + plane, train_recv.at[pl.ds(0, SPOTS)])
            for j in range(SLICE_ROWS):
                pairs = train_recv[plane * SPOTS : (plane + 1) * SPOTS, j // 2]
                pairs = pairs.reshape(SPOTS // 2, 2, TILE, LANES)
                even, odd = pairs[:, 0], pairs[:, 1]
                if j % 2 == 0:
                    rows = jnp.where(low, even, pltpu.roll(odd, trains, 1))
                else:
                    rows = jnp.where(low, pltpu.roll(even, trains, 1), odd)
                high_part, low_part = halves(rows.reshape(high, LANES))
                train_high[plane * high : (plane + 1) * high, j * LANES : (j + 1) * LANES] = high_part
                train_low[plane * high : (plane + 1) * high, j * LANES : (j + 1) * LANES] = low_part
        train_halves = train_high[...], train_low[...]
        gram_part[...] = product(train_halves, train_halves, 1)
        share = members * trains // SPOTS

        def send_part(to, device):
            send(2, gram_part.at[pl.ds(pl.multiple_of(to * share, share), share)], gram_recv.at[spot], device)

        to_others(send_part)

        gram_recv[spot] = gram_part[pl.ds(pl.multiple_of(spot * share, share), share), :]

        rest = pl.ds(0, SPOTS - 1)
        received(2, gram_recv.at[rest])
        gram_row[...] = jnp.sum(gram_recv[...], axis=0)
        my_rows = pl.ds(pl.multiple_of(spot * share, share), share)

        to_others(lambda to, device: send(4, gram_row, gram_full.at[my_rows], device))
        gram_full[my_rows, :] = gram_row[...]

        received(1, query_recv)
        planes = query_recv[...].reshape(PLANES, SPOTS, TILE, LANES)
        position = lax.broadcasted_iota(jnp.int32, (SPOTS, TILE, LANES), 1) // queries
        slices = []
        for j in range(SLICE_ROWS):
            rows = jnp.zeros((SPOTS, TILE, LANES), jnp.float32)
            for plane in range(PLANES):
                shift = (queries * (plane - j)) % TILE
                moved = pltpu.roll(planes[plane], shift, 1) if shift else planes[plane]
                rows = jnp.where(position == plane, moved, rows)
            slices.append(rows.reshape(SPOTS * TILE, LANES))
        cross = product(halves(jnp.concatenate(slices, axis=1)), (train_high[...], train_low[...]), 1)
        cross_part[...] = cross.reshape(SPOTS, TILE, LANES)

        to_others(lambda to, device: send(3, cross_part.at[to], cross_recv.at[spot], device))
        cross_recv[spot] = cross_part[spot]

        received(4, gram_full.at[pl.ds(0, share * (SPOTS - 1))])

        gram = gram_full[...]
        total = gram.shape[0]
        diagonal = lax.broadcasted_iota(jnp.int32, gram.shape, 0) == lax.broadcasted_iota(jnp.int32, gram.shape, 1)
        trace = jnp.sum(jnp.where(diagonal, gram, 0.0), axis=(0, 1), keepdims=True)
        ridge = RIDGE_SCALE * trace / total
        gram_full[...] = jnp.where(diagonal, gram + ridge, gram)

        def cross_terms():
            received(3, cross_recv.at[rest])
            return jnp.sum(cross_recv[...], axis=0)

        score_send[...] = solve(gram_full, steps, cross_terms)

        for around in (2, 1, 3, 0):
            for up in (2, 3, 1, 0):
                if around or up:
                    to = lax.rem(layer_here + up, layers) * RING + lax.rem(y + around, RING)
                    send(5, score_send, score_recv.at[mine], {"dp": dp, "mp": to})
        score_recv[mine] = score_send[...]
        received(5, score_recv.at[pl.ds(0, ckpts - 1)])
        scale = members * trains / ckpts
        summed = jnp.sum(score_recv[...], axis=0) * scale
        summed = pltpu.roll(summed, lax.rem((ckpts - mp) * width, LANES), 1)
        out_here[...] = summed[0:queries, 0:width]
        write.start()
        pl.semaphore_wait(reach_sem, PLANES - 1)
        for plane in range(1, PLANES):
            result_send[plane, 0:queries, :] = summed[plane * queries : (plane + 1) * queries]
            result_send[plane, queries:, :] = jnp.zeros((TILE - queries, LANES), jnp.float32)
            send(6, result_send.at[plane], result_recv, {"dp": plane * SPOTS + spot, "mp": mp})
        sent(2, gram_recv.at[rest])
        sent(3, cross_recv.at[rest])
        sent(4, gram_full.at[pl.ds(0, share * (SPOTS - 1))])
        sent(5, score_recv.at[pl.ds(0, ckpts - 1)])
        sent(6, result_send.at[pl.ds(0, PLANES - 1)])

    @pl.when(jnp.logical_not(home))
    def _():
        received(6, result_recv)
        out_here[...] = result_recv[0:queries, 0:width]
        write.start()

    write.wait()
    sent(1, query_row)
    sent(QUERY_ROW, query_send.at[pl.ds(0, SPOTS - 1)])


def shards(train_acts, train_grads, query_acts, query_grads, train_lengths, query_lengths, proj_salts):
    _, trains, length, width = train_acts.shape
    queries, out_width = query_acts.shape[1], train_grads.shape[3]
    members, ckpts = lax.axis_size("dp"), lax.axis_size("mp")
    total = trains * members
    f32, bf16 = jnp.float32, jnp.bfloat16
    i32 = jnp.int32
    return pl.pallas_call(
        kernel,
        out_shape=jax.ShapeDtypeStruct((queries, total // ckpts), f32),
        in_specs=[pl.BlockSpec(memory_space=pltpu.HBM)] * 7,
        out_specs=pl.BlockSpec(memory_space=pltpu.HBM),
        scratch_shapes=[
            pltpu.VMEM((trains + queries, length, width), bf16),
            pltpu.VMEM((trains + queries, length, out_width), bf16),
            pltpu.VMEM((width // 2, LANES), bf16),
            pltpu.VMEM((out_width // 2, LANES), bf16),
            pltpu.VMEM((SPOTS, SLICE_ROWS // 2, TILE, LANES), f32),
            pltpu.VMEM((SPOTS, TILE, LANES), f32),
            pltpu.VMEM((SPOTS, TILE, LANES), f32),
            pltpu.VMEM((members, SLICE_ROWS // 2, TILE, LANES), f32),
            pltpu.VMEM((members, TILE, LANES), f32),
            pltpu.VMEM((total, SLICE_ROWS * LANES), bf16),
            pltpu.VMEM((total, SLICE_ROWS * LANES), bf16),
            pltpu.VMEM((total, LANES), f32),
            pltpu.VMEM((SPOTS, TILE, LANES), f32),
            pltpu.VMEM((SPOTS, total // SPOTS, LANES), f32),
            pltpu.VMEM((SPOTS, TILE, LANES), f32),
            pltpu.VMEM((total // SPOTS, LANES), f32),
            pltpu.VMEM((total, LANES), f32),
            pltpu.VMEM((total, LANES), f32),
            pltpu.VMEM((TILE, LANES), f32),
            pltpu.VMEM((ckpts, TILE, LANES), f32),
            pltpu.VMEM((PLANES, TILE, LANES), f32),
            pltpu.VMEM((TILE, LANES), f32),
            pltpu.VMEM((queries, total // ckpts), f32),
            pltpu.VMEM((2, trains * length, LANES), f32),
            pltpu.SMEM((1, 2), i32),
            pltpu.SMEM((trains,), i32),
            pltpu.SMEM((queries,), i32),
            pltpu.SemaphoreType.DMA((9,)),
            pltpu.SemaphoreType.DMA((QUERY_ROW + 1,)),
            pltpu.SemaphoreType.DMA((QUERY_ROW + 1 + PLANES,)),
            pltpu.SemaphoreType.REGULAR,
            pltpu.SemaphoreType.REGULAR,
            pltpu.SemaphoreType.REGULAR,
        ],
        compiler_params=pltpu.CompilerParams(
            collective_id=0, has_side_effects=True, vmem_limit_bytes=64 * 1024 * 1024
        ),
    )(proj_salts, train_lengths, query_lengths, train_acts, train_grads, query_acts, query_grads)


def solution(mesh):
    placed = (
        P("mp", "dp", None, None),
        P("mp", "dp", None, None),
        P("mp", "dp", None, None),
        P("mp", "dp", None, None),
        P("dp"),
        P("dp"),
        P("mp", None),
    )
    return jax.shard_map(shards, mesh=mesh, in_specs=placed, out_specs=P("dp", "mp"), check_vma=False)
```

```python
import functools

import jax
import jax.numpy as jnp
from jax import lax
from jax.experimental import pallas as pl
from jax.experimental.pallas import tpu as pltpu
from jax.sharding import PartitionSpec as P

MESH = pl.DeviceIdType.MESH
R1 = 64
R2 = 64
RIDGE_SCALE = 0.1
LANES = 128
TILE = 8
RING = 4
PLANES = 4
QUERY_ROW = 7
SPOTS = 8
CORES = 2
LATE = 6
PIVOTS = 16
SLICE_ROWS = 4


def sign_table(salt, rows, table_ref):
    half = rows // 2
    row = lax.broadcasted_iota(jnp.int32, (LANES, LANES), 0)
    lane = lax.broadcasted_iota(jnp.int32, (LANES, LANES), 1)
    row = row + jnp.where(lane >= R1, half, 0)
    base = row * 73856093 + (lane & (R1 - 1)) * 19349663 + salt * 83492791
    scale = 1.0 / rows**0.5

    def chunk(step, carry):
        h = base + step * LANES * 73856093
        h = h ^ lax.shift_right_logical(h, 15)
        h = h * 1274126177
        h = h ^ lax.shift_right_logical(h, 13)
        h = h * 668265263
        bit = (lax.shift_right_logical(h, 16) ^ h) & 128
        signs = jnp.where(bit != 0, scale, -scale).astype(jnp.bfloat16)
        table_ref[pl.ds(pl.multiple_of(step * LANES, LANES), LANES), :] = signs
        return carry

    lax.fori_loop(0, half // LANES, chunk, 0, unroll=2)


def projected(tokens, table):
    half = table.shape[0]
    upper = jnp.dot(tokens[:, :half], table, preferred_element_type=jnp.float32)
    lower = jnp.dot(tokens[:, half:], table, preferred_element_type=jnp.float32)
    return upper[:, :R1] + lower[:, R1:]


def halves(values):
    high = values.astype(jnp.bfloat16)
    return high, (values - high.astype(jnp.float32)).astype(jnp.bfloat16)


def product(first, second, axis):
    (first_high, first_low), (second_high, second_low) = first, second
    return lax.dot_general(
        jnp.concatenate([first_high, first_high, first_low], axis=axis),
        jnp.concatenate([second_high, second_low, second_high], axis=axis),
        (((axis,), (axis,)), ((), ())),
        preferred_element_type=jnp.float32,
    )


def features(left, right, length):
    position = lax.broadcasted_iota(jnp.int32, left.shape, 0)
    left = jnp.where(position < length, left, 0.0)
    outer = product(halves(left), halves(right), 0)
    return jnp.concatenate([outer[: R1 // 2], outer[R1 // 2 :]], axis=1)


def solve(system_ref, steps_ref, late_rhs):
    total = system_ref.shape[0]
    high = PIVOTS // TILE
    sublane = lax.broadcasted_iota(jnp.int32, (TILE, LANES), 0)
    lane = lax.broadcasted_iota(jnp.int32, (TILE, LANES), 1)

    def spread(tile, column):
        return jnp.broadcast_to(tile[:, column : column + 1], (TILE, LANES))

    def down(tile, row):
        return jnp.broadcast_to(tile[row : row + 1, :], (TILE, LANES))

    def eliminate(tile, start, rows):
        inside = (lane >= start) & (lane < start + PIVOTS)
        terms = [spread(tile, start + t) * down(rows[t // TILE], t % TILE) for t in range(PIVOTS)]
        while len(terms) > 1:
            terms = [a + b for a, b in zip(terms[::2], terms[1::2])]
        return jnp.where(inside, 0.0, tile) - terms[0]

    def rows_at(ref, first, count):
        return [ref[TILE * b : TILE * (b + 1), :] for b in range(first, first + count)]

    tiles = rows_at(system_ref, 0, total // TILE)
    rhs = None
    for start in range(0, total, PIVOTS):
        first = start // TILE
        if start == LATE * PIVOTS:
            for b in range(first, len(tiles)):
                system_ref[TILE * b : TILE * (b + 1), :] = tiles[b]
            rhs = late_rhs()
            tiles[first:] = rows_at(system_ref, first, len(tiles) - first)
            for done in range(0, start, PIVOTS):
                rhs = eliminate(rhs, done, rows_at(steps_ref, done // TILE, high))
        inside = (lane >= start) & (lane < start + PIVOTS)
        block = tiles[first : first + high]
        columns = [[spread(tile, start + t) for tile in block] for t in range(PIVOTS)]
        rows = [
            jnp.where(inside, jnp.where(lane - start == sublane + TILE * g, -1.0, 0.0), block[g]) for g in range(high)
        ]
        for t in range(PIVOTS):
            g, r = t // TILE, t % TILE
            here = sublane == r
            scale = 1.0 / down(columns[t][g], r)
            pivot_row = down(rows[g], r) * scale
            rows = [rows[i] - columns[t][i] * pivot_row for i in range(high)]
            rows[g] = jnp.where(here, pivot_row, rows[g])
            for c in range(t + 1, PIVOTS):
                scaled = down(columns[c][g], r) * scale
                column = [columns[c][i] - columns[t][i] * scaled for i in range(high)]
                column[g] = jnp.where(here, scaled, column[g])
                columns[c] = column
        for i in range(first + high, len(tiles)):
            tiles[i] = eliminate(tiles[i], start, rows)
        if rhs is not None:
            rhs = eliminate(rhs, start, rows)
        elif start < LATE * PIVOTS:
            for g in range(high):
                steps_ref[TILE * (first + g) : TILE * (first + g + 1), :] = rows[g]
    return rhs


def kernel(
    salts, train_lengths, query_lengths, train_acts, train_grads, query_acts, query_grads, out_ref,
    acts, grads, table_in, table_out, train_send, query_send, query_row, train_recv, query_recv, train_high, train_low,
    gram_part, cross_part, gram_recv, cross_recv, gram_row, gram_full, steps, score_send, score_recv, result_send, result_recv,
    out_here, projections, salts_here, train_lengths_here, query_lengths_here, load_sems, send_sems, recv_sems, here_sem, go_sem, reach_sem,
):
    dp, mp = lax.axis_index("dp"), lax.axis_index("mp")
    members, ckpts = lax.axis_size("dp"), lax.axis_size("mp")
    trains, queries = train_acts.shape[1], query_acts.shape[1]
    spot = lax.rem(dp, SPOTS)
    plane_here, layer_here = dp // SPOTS, mp // RING
    y = lax.rem(mp, RING)
    layers = ckpts // RING
    home = plane_here == 0
    mine = (layer_here + layers - 1) % layers * RING + y
    last = layers - 1
    late = plane_here == PLANES - 2
    tail_up = (plane_here == PLANES - 1) & (layer_here == last)
    yields_up = (plane_here == PLANES - 1) & (layer_here < last) | late & (layer_here == last)
    tail_down = late & (layer_here == 0)
    yields_down = late & (layer_here > 0) & (layer_here < last)
    tail, yields = tail_up | tail_down, yields_up | yields_down
    awaited = jnp.where(tail_up, layers, jnp.where(tail_down, layers - 2, 0))
    tail_of_mine = {
        "dp": (PLANES - 2 + yields_up.astype(jnp.int32)) * SPOTS + spot,
        "mp": jnp.where(yields_up, last, 0) * RING + y,
    }

    def before(k):
        up = {"plane": PLANES - 1 - k // last, "layer": k}
        down = {"plane": PLANES - 2, "layer": k + 1}
        plane, layer = (jnp.where(tail_up, up[name], down[name]) for name in ("plane", "layer"))
        return {"dp": plane * SPOTS + spot, "mp": layer * RING + y}

    home_of_mine = (layer_here + 1) % layers * RING + y

    half = acts.shape[2] // 2
    first_half, second_half = pl.ds(0, half), pl.ds(half, half)
    small = [
        pltpu.make_async_copy(salts, salts_here, load_sems.at[4]),
        pltpu.make_async_copy(train_lengths, train_lengths_here, load_sems.at[5]),
        pltpu.make_async_copy(query_lengths, query_lengths_here, load_sems.at[6]),
    ]
    loads = [
        pltpu.make_async_copy(train_grads.at[0], grads.at[pl.ds(0, trains)], load_sems.at[0]),
        pltpu.make_async_copy(train_acts.at[0, :, :, first_half], acts.at[pl.ds(0, trains), :, first_half], load_sems.at[1]),
        pltpu.make_async_copy(query_grads.at[0], grads.at[pl.ds(trains, queries)], load_sems.at[2]),
        pltpu.make_async_copy(query_acts.at[0], acts.at[pl.ds(trains, queries)], load_sems.at[3]),
        pltpu.make_async_copy(train_acts.at[0, :, :, second_half], acts.at[pl.ds(0, trains), :, second_half], load_sems.at[7]),
    ]
    for load in [*small, *loads[:2], loads[4]]:
        load.start()

    barrier = pltpu.get_barrier_semaphore()

    def greet(peer):
        pl.semaphore_signal(barrier, inc=1, device_id=peer, device_id_type=MESH)

    def send(phase, source, target, device, arrival=None):
        copy = pltpu.make_async_remote_copy(
            src_ref=source, dst_ref=target, send_sem=send_sems.at[phase],
            recv_sem=recv_sems.at[phase if arrival is None else arrival], device_id=device, device_id_type=MESH,
        )
        copy.start()

    def sent(phase, like):
        pltpu.make_async_copy(like, like, send_sems.at[phase]).wait()

    def received(phase, like):
        pltpu.make_async_copy(like, like, recv_sems.at[phase]).wait()

    @pl.when(home)
    def _():
        @pl.loop(0, members)
        def _(k):
            greet({"dp": k, "mp": mine})

        @pl.loop(1, ckpts)
        def _(k):
            greet({"dp": dp, "mp": lax.rem(mp + k, ckpts)})

        for plane in range(1, PLANES):
            greet({"dp": plane * SPOTS + spot, "mp": mp})

    @pl.loop(1, SPOTS)
    def _(k):
        greet({"dp": plane_here * SPOTS + lax.rem(spot + k, SPOTS), "mp": mp})

    @pl.when(tail)
    def _():
        @pl.loop(0, awaited)
        def _(k):
            greet(before(k))

    small[0].wait()
    sign_table(salts_here[0, 1], grads.shape[2], table_out)
    sign_table(salts_here[0, 0], acts.shape[2], table_in)

    length, width = acts.shape[1], out_ref.shape[1]
    write = pltpu.make_async_copy(out_here, out_ref, load_sems.at[8])

    def example_features(first, count):
        some = pl.ds(first, count)
        right = projected(grads[some].reshape(count * length, grads.shape[2]), table_out[...])
        if first == 0:
            projections[0, :, 0:R2] = right
            loads[1].wait()
            tokens = acts[some, :, first_half].reshape(count * length, half)
            projections[1] = jnp.dot(tokens, table_in[...], preferred_element_type=jnp.float32)
            loads[4].wait()
            tokens = acts[some, :, second_half].reshape(count * length, half)
            left = jnp.dot(tokens, table_in[...], preferred_element_type=jnp.float32)
            left = projections[1, :, 0:R1] + left[:, R1:]
            right = projections[0, :, 0:R2]
        else:
            loads[3].wait()
            left = projected(acts[some].reshape(count * length, acts.shape[2]), table_in[...])
        for e in range(count):
            tokens = slice(e * length, (e + 1) * length)
            used = train_lengths_here[e] if first == 0 else query_lengths_here[e]
            yield e, features(left[tokens], right[tokens], used).reshape(SPOTS, SLICE_ROWS, LANES)

    small[1].wait()
    small[2].wait()
    loads[0].wait()
    loads[2].start()
    loads[3].start()
    for e, rows in example_features(0, trains):
        for j in range(SLICE_ROWS):
            train_send[:, j // 2, (j % 2) * trains + e, :] = rows[:, j]

    pl.semaphore_wait(barrier, 2 * SPOTS - 1 + jnp.where(home, ckpts - 1, 1) + yields.astype(jnp.int32))

    @pl.when(jnp.logical_not(home))
    def _():
        pl.semaphore_signal(reach_sem, inc=1, device_id={"dp": spot, "mp": mp}, device_id_type=MESH)

    @pl.when(yields)
    def _():
        pl.semaphore_signal(here_sem, inc=1, device_id=tail_of_mine, device_id_type=MESH)


    def to_others(action):
        x, core, chips = spot // CORES, lax.rem(spot, CORES), SPOTS // CORES
        for away, other in ((2, 0), (2, 1), (1, 0), (1, 1), (3, 0), (3, 1), (0, 1)):
            to = lax.rem(x + away, chips) * CORES + lax.rem(core + other, CORES)
            action(to, {"dp": plane_here * SPOTS + to, "mp": mp})

    @pl.loop(0, SPOTS)
    def _(k):
        to = lax.rem(spot + k, SPOTS)
        there = {"dp": to, "mp": home_of_mine}
        send(0, train_send.at[to], train_recv.at[dp], there, arrival=QUERY_ROW + 1 + plane_here)

    loads[2].wait()
    for e, rows in example_features(trains, queries):
        for j in range(SLICE_ROWS):
            query_send[:, j * queries + e, :] = rows[:, j]
    to_others(lambda to, device: send(QUERY_ROW, query_send.at[to], query_row.at[spot], device))
    query_row[spot] = query_send[spot]
    received(QUERY_ROW, query_row.at[pl.ds(0, SPOTS - 1)])
    sent(0, train_send)

    @pl.when(tail)
    def _():
        pl.semaphore_wait(here_sem, awaited)

        @pl.loop(0, awaited)
        def _(k):
            pl.semaphore_signal(go_sem, inc=1, device_id=before(k), device_id_type=MESH)

    @pl.when(yields)
    def _():
        pl.semaphore_wait(go_sem, 1)

    in_plane = pl.ds(pl.multiple_of(plane_here * SPOTS, SPOTS), SPOTS)
    send(1, query_row, query_recv.at[in_plane], {"dp": spot, "mp": home_of_mine})

    @pl.when(home)
    def _():
        low = lax.broadcasted_iota(jnp.int32, (SPOTS // 2, TILE, LANES), 1) < trains
        high = SPOTS * trains
        for plane in range(PLANES):
            if plane == PLANES - 1:
                known = plane * high
                earlier = train_high[0:known, :], train_low[0:known, :]
                gram_part[0:known, 0:known] = product(earlier, earlier, 1)
            received(QUERY_ROW + 1 + plane, train_recv.at[pl.ds(0, SPOTS)])
            for j in range(SLICE_ROWS):
                pairs = train_recv[plane * SPOTS : (plane + 1) * SPOTS, j // 2]
                pairs = pairs.reshape(SPOTS // 2, 2, TILE, LANES)
                even, odd = pairs[:, 0], pairs[:, 1]
                if j % 2 == 0:
                    rows = jnp.where(low, even, pltpu.roll(odd, trains, 1))
                else:
                    rows = jnp.where(low, pltpu.roll(even, trains, 1), odd)
                high_part, low_part = halves(rows.reshape(high, LANES))
                train_high[plane * high : (plane + 1) * high, j * LANES : (j + 1) * LANES] = high_part
                train_low[plane * high : (plane + 1) * high, j * LANES : (j + 1) * LANES] = low_part
        train_halves = train_high[...], train_low[...]
        latest = train_high[known:, :], train_low[known:, :]
        gram_part[known:, :] = product(latest, train_halves, 1)
        gram_part[0:known, known:] = product((train_high[0:known, :], train_low[0:known, :]), latest, 1)
        share = members * trains // SPOTS

        def send_part(to, device):
            send(2, gram_part.at[pl.ds(pl.multiple_of(to * share, share), share)], gram_recv.at[spot], device)

        to_others(send_part)

        gram_recv[spot] = gram_part[pl.ds(pl.multiple_of(spot * share, share), share), :]

        rest = pl.ds(0, SPOTS - 1)
        received(2, gram_recv.at[rest])
        gram_row[...] = jnp.sum(gram_recv[...], axis=0)
        my_rows = pl.ds(pl.multiple_of(spot * share, share), share)

        to_others(lambda to, device: send(4, gram_row, gram_full.at[my_rows], device))
        gram_full[my_rows, :] = gram_row[...]

        received(1, query_recv)
        planes = query_recv[...].reshape(PLANES, SPOTS, TILE, LANES)
        position = lax.broadcasted_iota(jnp.int32, (SPOTS, TILE, LANES), 1) // queries
        slices = []
        for j in range(SLICE_ROWS):
            rows = jnp.zeros((SPOTS, TILE, LANES), jnp.float32)
            for plane in range(PLANES):
                shift = (queries * (plane - j)) % TILE
                moved = pltpu.roll(planes[plane], shift, 1) if shift else planes[plane]
                rows = jnp.where(position == plane, moved, rows)
            slices.append(rows.reshape(SPOTS * TILE, LANES))
        cross = product(halves(jnp.concatenate(slices, axis=1)), (train_high[...], train_low[...]), 1)
        cross_part[...] = cross.reshape(SPOTS, TILE, LANES)

        to_others(lambda to, device: send(3, cross_part.at[to], cross_recv.at[spot], device))
        cross_recv[spot] = cross_part[spot]

        received(4, gram_full.at[pl.ds(0, share * (SPOTS - 1))])

        gram = gram_full[...]
        total = gram.shape[0]
        diagonal = lax.broadcasted_iota(jnp.int32, gram.shape, 0) == lax.broadcasted_iota(jnp.int32, gram.shape, 1)
        trace = jnp.sum(jnp.where(diagonal, gram, 0.0), axis=(0, 1), keepdims=True)
        ridge = RIDGE_SCALE * trace / total
        gram_full[...] = jnp.where(diagonal, gram + ridge, gram)

        def cross_terms():
            received(3, cross_recv.at[rest])
            return jnp.sum(cross_recv[...], axis=0)

        score_send[...] = solve(gram_full, steps, cross_terms)

        for around in (2, 1, 3, 0):
            for up in (2, 3, 1, 0):
                if around or up:
                    to = lax.rem(layer_here + up, layers) * RING + lax.rem(y + around, RING)
                    send(5, score_send, score_recv.at[mine], {"dp": dp, "mp": to})
        score_recv[mine] = score_send[...]
        received(5, score_recv.at[pl.ds(0, ckpts - 1)])
        scale = members * trains / ckpts
        summed = jnp.sum(score_recv[...], axis=0) * scale
        summed = pltpu.roll(summed, lax.rem((ckpts - mp) * width, LANES), 1)
        out_here[...] = summed[0:queries, 0:width]
        write.start()
        pl.semaphore_wait(reach_sem, PLANES - 1)
        for plane in range(1, PLANES):
            result_send[plane, 0:queries, :] = summed[plane * queries : (plane + 1) * queries]
            result_send[plane, queries:, :] = jnp.zeros((TILE - queries, LANES), jnp.float32)
            send(6, result_send.at[plane], result_recv, {"dp": plane * SPOTS + spot, "mp": mp})
        sent(2, gram_recv.at[rest])
        sent(3, cross_recv.at[rest])
        sent(4, gram_full.at[pl.ds(0, share * (SPOTS - 1))])
        sent(5, score_recv.at[pl.ds(0, ckpts - 1)])
        sent(6, result_send.at[pl.ds(0, PLANES - 1)])

    @pl.when(jnp.logical_not(home))
    def _():
        received(6, result_recv)
        out_here[...] = result_recv[0:queries, 0:width]
        write.start()

    write.wait()
    sent(1, query_row)
    sent(QUERY_ROW, query_send.at[pl.ds(0, SPOTS - 1)])


def shards(train_acts, train_grads, query_acts, query_grads, train_lengths, query_lengths, proj_salts):
    _, trains, length, width = train_acts.shape
    queries, out_width = query_acts.shape[1], train_grads.shape[3]
    members, ckpts = lax.axis_size("dp"), lax.axis_size("mp")
    total = trains * members
    f32, bf16 = jnp.float32, jnp.bfloat16
    i32 = jnp.int32
    return pl.pallas_call(
        kernel,
        out_shape=jax.ShapeDtypeStruct((queries, total // ckpts), f32),
        in_specs=[pl.BlockSpec(memory_space=pltpu.HBM)] * 7,
        out_specs=pl.BlockSpec(memory_space=pltpu.HBM),
        scratch_shapes=[
            pltpu.VMEM((trains + queries, length, width), bf16),
            pltpu.VMEM((trains + queries, length, out_width), bf16),
            pltpu.VMEM((width // 2, LANES), bf16),
            pltpu.VMEM((out_width // 2, LANES), bf16),
            pltpu.VMEM((SPOTS, SLICE_ROWS // 2, TILE, LANES), f32),
            pltpu.VMEM((SPOTS, TILE, LANES), f32),
            pltpu.VMEM((SPOTS, TILE, LANES), f32),
            pltpu.VMEM((members, SLICE_ROWS // 2, TILE, LANES), f32),
            pltpu.VMEM((members, TILE, LANES), f32),
            pltpu.VMEM((total, SLICE_ROWS * LANES), bf16),
            pltpu.VMEM((total, SLICE_ROWS * LANES), bf16),
            pltpu.VMEM((total, LANES), f32),
            pltpu.VMEM((SPOTS, TILE, LANES), f32),
            pltpu.VMEM((SPOTS, total // SPOTS, LANES), f32),
            pltpu.VMEM((SPOTS, TILE, LANES), f32),
            pltpu.VMEM((total // SPOTS, LANES), f32),
            pltpu.VMEM((total, LANES), f32),
            pltpu.VMEM((total, LANES), f32),
            pltpu.VMEM((TILE, LANES), f32),
            pltpu.VMEM((ckpts, TILE, LANES), f32),
            pltpu.VMEM((PLANES, TILE, LANES), f32),
            pltpu.VMEM((TILE, LANES), f32),
            pltpu.VMEM((queries, total // ckpts), f32),
            pltpu.VMEM((2, trains * length, LANES), f32),
            pltpu.SMEM((1, 2), i32),
            pltpu.SMEM((trains,), i32),
            pltpu.SMEM((queries,), i32),
            pltpu.SemaphoreType.DMA((9,)),
            pltpu.SemaphoreType.DMA((QUERY_ROW + 1,)),
            pltpu.SemaphoreType.DMA((QUERY_ROW + 1 + PLANES,)),
            pltpu.SemaphoreType.REGULAR,
            pltpu.SemaphoreType.REGULAR,
            pltpu.SemaphoreType.REGULAR,
        ],
        compiler_params=pltpu.CompilerParams(
            collective_id=0, has_side_effects=True, vmem_limit_bytes=64 * 1024 * 1024
        ),
    )(proj_salts, train_lengths, query_lengths, train_acts, train_grads, query_acts, query_grads)


def solution(mesh):
    placed = (
        P("mp", "dp", None, None),
        P("mp", "dp", None, None),
        P("mp", "dp", None, None),
        P("mp", "dp", None, None),
        P("dp"),
        P("dp"),
        P("mp", None),
    )
    return jax.shard_map(shards, mesh=mesh, in_specs=placed, out_specs=P("dp", "mp"), check_vma=False)
```
